32 devices in a mesh: sec: 2 (over core), grp: 16 (over z, y, x).
Axes of the slice: x: 2, y: 2, z: 4, core: 2. Of those that a mesh axis runs over, the one named last changes fastest.
Arguments:
- stratum_warmth_anomaly: float32 [90, 8192], P('sec', 'grp'), may hold values from 0.7 to 1.3
- pressure_depth: float32 [90, 8192], P('sec', 'grp'), may hold values from 0.5 to 2
- absorber_amounts: float32 [4, 90, 8192], P(None, 'sec', 'grp'), may hold values from 0.1 to 1
- ground_warmth_anomaly: float32 [8192], P('grp'), may hold values from 0.9 to 1.3
- sun_elevation_factor: float32 [8192], P('grp'), may hold values from 0.2 to 1
- daytime_mask: int32 [8192], P('grp'), may hold values 0 or 1
- dispatch_position: int32 [16, 512], P('grp'), may hold values from 0 to 511, each once within a row
- arrival_membership: int32 [16, 512], P('grp'), may hold values from 0 to 511, each once within a row
- adjacency_table: int32 [6, 8192], P(None, 'grp'), may hold values from 0 to 639, as said below
- blending_coefficient: float32 [6, 8192], P(None, 'grp'), may hold values from 0.02 to 0.15
- opacity_table: float32 [4, 112, 90], P(None, 'sec'), may hold values from 0.001 to 0.3
- emission_share: float32 [112], P('sec'), may hold values from 0.05 to 0.5
- sunshine_share: float32 [112], P('sec'), may hold values from 0.05 to 0.5
Outputs:
- heating: float32 [90, 8192], P('sec', 'grp')
- mixed: float32 [4, 90, 8192], P(None, 'sec', 'grp')
The draws below stay inside these ranges and needn't reach their ends.
Inputs may be any that keep to these rules, and one draw needn't show every extreme that they name: `dispatch_position`: each row is a permutation of 0 to 511. `arrival_membership`: each row is a permutation of 0 to 511, so every radiation column has exactly four members. adjacency_table[k, c] - (c mod 512) lies in 0 to 128.
All inputs are finite; a program needn't handle non-finite values. No bound on the sum of `daytime_mask` on one device may be relied on, other than what follows from the above.
Results may differ from the reference program's by a relative error of at most 0.0003.
Values sent between devices are 32-bit elements; how exact they have to be, the bound alone decides.
A program may use at most 64 MiB of HBM per device.

```python
import math
import jax
import jax.numpy as jnp
from jax import lax

COL_DEV = 512
LAYER_TALLY = 90
GPTS = 112
SPECIES = 4
NEAR_COUNT = 6
STEPS = 4
LEVEL_BLOCK = 9
HALO = 64
GRID_CELL_TALLY = 8192
N_GRP = 16


def draw_adjacency_table(key, part):
    local_ids = jnp.arange(GRID_CELL_TALLY, dtype=jnp.int32) % COL_DEV
    offsets = jax.random.randint(key, (NEAR_COUNT, GRID_CELL_TALLY), -HALO, HALO + 1, dtype=jnp.int32)
    row_ids = jnp.arange(NEAR_COUNT, dtype=jnp.int32)[:, None]
    offsets = jnp.where((row_ids == 0) & (local_ids[None, :] == COL_DEV - 1), HALO, offsets)
    offsets = jnp.where((row_ids == 1) & (local_ids[None, :] == 0), -HALO, offsets)
    return local_ids[None, :] + HALO + offsets


def with_ends(result, own_key, low, high):
    shape = result.shape
    spot = [jax.random.randint(jax.random.fold_in(own_key, axis), (), 0, shape[axis]) for axis in range(len(shape))]
    result = result.at[tuple(spot)].set(low)
    longest = shape.index(max(shape))
    spot[longest] = (spot[longest] + 1) % shape[longest]
    return result.at[tuple(spot)].set(high)


def shard_levels(own_key, shape, cuts, least, largest):
    level, own = 1.0, jax.random.fold_in(own_key, 6)
    for dim, parts in cuts:
        steps = jnp.exp(jax.random.uniform(jax.random.fold_in(own, dim), (parts,), jnp.float32, least / len(cuts), largest / len(cuts)))
        level = level * jnp.repeat(steps, shape[dim] // parts).reshape([-1 if axis == dim else 1 for axis in range(len(shape))])
    return level


def setup_inputs(seed: int = 0) -> dict:
    key_list = jax.random.split(jax.random.key(seed), 14)
    stratum_warmth_anomaly = jnp.clip(0.7 + 0.59999996 * jax.random.uniform(key_list[0], (LAYER_TALLY, GRID_CELL_TALLY), jnp.float32) ** shard_levels(key_list[0], (LAYER_TALLY, GRID_CELL_TALLY), ((0, 2), (1, 16)), -0.2, 0.2), 0.7, 1.3)
    pressure_depth = jnp.clip(0.5 + 1.5 * jax.random.uniform(key_list[1], (LAYER_TALLY, GRID_CELL_TALLY), jnp.float32) ** shard_levels(key_list[1], (LAYER_TALLY, GRID_CELL_TALLY), ((0, 2), (1, 16)), -0.2, 0.2), 0.5, 2.0)
    absorber_amounts = jnp.clip(jnp.exp(math.log(1.0) - 2.3025851 * jax.random.uniform(key_list[2], (SPECIES, LAYER_TALLY, GRID_CELL_TALLY), jnp.float32) ** shard_levels(key_list[2], (SPECIES, LAYER_TALLY, GRID_CELL_TALLY), ((1, 2), (2, 16)), -0.2, 0.2)), 0.1, 1.0)
    ground_warmth_anomaly = jnp.clip(0.9 + 0.39999998 * jax.random.uniform(key_list[3], (GRID_CELL_TALLY,), jnp.float32) ** shard_levels(key_list[3], (GRID_CELL_TALLY,), ((0, 16),), -0.2, 0.2), 0.9, 1.3)
    sun_elevation_factor = jnp.clip(0.2 + 0.8 * jax.random.uniform(key_list[4], (GRID_CELL_TALLY,), jnp.float32) ** shard_levels(key_list[4], (GRID_CELL_TALLY,), ((0, 16),), -0.2, 0.2), 0.2, 1.0)
    daytime_mask = with_ends((jax.random.randint(key_list[5], (GRID_CELL_TALLY,), 0, 2) < 1).astype(jnp.int32), jax.random.fold_in(key_list[5], 1), 0, 1)
    dispatch_position = jax.vmap(lambda own: jax.random.permutation(own, COL_DEV))(jax.random.split(key_list[6], N_GRP)).reshape((N_GRP, COL_DEV)).astype(jnp.int32)
    arrival_membership = jax.vmap(lambda own: jax.random.permutation(own, COL_DEV))(jax.random.split(key_list[7], N_GRP)).reshape((N_GRP, COL_DEV)).astype(jnp.int32)
    adjacency_table = draw_adjacency_table(jax.random.fold_in(key_list[13], 71), 0)
    blending_coefficient = jnp.clip(jnp.exp(math.log(0.15) - 2.014903 * jax.random.uniform(key_list[9], (NEAR_COUNT, GRID_CELL_TALLY), jnp.float32) ** shard_levels(key_list[9], (NEAR_COUNT, GRID_CELL_TALLY), ((1, 16),), -0.2, 0.2)), 0.02, 0.15)
    opacity_table = jnp.clip(jnp.exp(math.log(0.3) - 5.7037825 * jax.random.uniform(key_list[10], (SPECIES, GPTS, LAYER_TALLY), jnp.float32) ** shard_levels(key_list[10], (SPECIES, GPTS, LAYER_TALLY), ((1, 2),), -0.2, 0.2)), 0.001, 0.3)
    emission_share = jnp.clip(jnp.exp(math.log(0.5) - 2.3025851 * jax.random.uniform(key_list[11], (GPTS,), jnp.float32) ** shard_levels(key_list[11], (GPTS,), ((0, 2),), -0.2, 0.2)), 0.05, 0.5)
    sunshine_share = jnp.clip(jnp.exp(math.log(0.5) - 2.3025851 * jax.random.uniform(key_list[12], (GPTS,), jnp.float32) ** shard_levels(key_list[12], (GPTS,), ((0, 2),), -0.2, 0.2)), 0.05, 0.5)
    return {"stratum_warmth_anomaly": stratum_warmth_anomaly, "pressure_depth": pressure_depth, "absorber_amounts": absorber_amounts, "ground_warmth_anomaly": ground_warmth_anomaly, "sun_elevation_factor": sun_elevation_factor, "daytime_mask": daytime_mask, "dispatch_position": dispatch_position, "arrival_membership": arrival_membership, "adjacency_table": adjacency_table, "blending_coefficient": blending_coefficient, "opacity_table": opacity_table, "emission_share": emission_share, "sunshine_share": sunshine_share}


DIFFUSE = 1.66


def optical(opacity_table, radiant_species, stratum_index):
    coeffs = lax.dynamic_index_in_dim(opacity_table, stratum_index, 2, keepdims=False)
    amounts = lax.dynamic_index_in_dim(radiant_species, stratum_index, 1, keepdims=False)
    optical_depth = coeffs[0][:, None] * amounts[0][None, :]
    for species in range(1, coeffs.shape[0]):
        optical_depth = optical_depth + coeffs[species][:, None] * amounts[species][None, :]
    return optical_depth


def compute_flux_heating(radiant_warmth, radiant_depth, radiant_species, radiant_ground, sunlight_incline, incoming_sunshine, opacity_table, emission_share, sunshine_share):
    strata_range, radiant_span = radiant_warmth.shape
    blocks = strata_range // LEVEL_BLOCK
    gpoints = emission_share.shape[0]
    block_ids = jnp.arange(blocks, dtype=jnp.int32)

    def layer_terms(stratum_index):
        optical_depth = optical(opacity_table, radiant_species, stratum_index)
        stratum_warmth = lax.dynamic_index_in_dim(radiant_warmth, stratum_index, 0, keepdims=False)
        source = emission_share[:, None] * (stratum_warmth ** 4)[None, :]
        return optical_depth, jnp.exp(-DIFFUSE * optical_depth), source

    def down_block(fluxes, block_id):
        thermal, direct = fluxes
        thermal_rows = []
        direct_rows = []
        for inner_id in range(LEVEL_BLOCK):
            optical_depth, transmit, source = layer_terms(block_id * LEVEL_BLOCK + inner_id)
            thermal = transmit * thermal + (1.0 - transmit) * source
            direct = direct * jnp.exp(-optical_depth / sunlight_incline[None, :])
            thermal_rows.append(jnp.sum(thermal, axis=0))
            direct_rows.append(jnp.sum(direct, axis=0))
        return (thermal, direct), (jnp.stack(thermal_rows), jnp.stack(direct_rows))

    down_init = (jnp.zeros((gpoints, radiant_span), jnp.float32), sunshine_share[:, None] * incoming_sunshine[None, :])
    final_down, (down_rows, direct_rows) = lax.scan(down_block, down_init, block_ids)
    thermal_down = jnp.concatenate([jnp.zeros((1, radiant_span), jnp.float32), down_rows.reshape(strata_range, radiant_span)], axis=0)
    direct_down = jnp.concatenate([jnp.sum(down_init[1], axis=0)[None], direct_rows.reshape(strata_range, radiant_span)], axis=0)

    def up_block(upward, block_id):
        upward_rows = []
        for inner_id in range(LEVEL_BLOCK - 1, -1, -1):
            optical_depth, transmit, source = layer_terms(block_id * LEVEL_BLOCK + inner_id)
            upward = transmit * upward + (1.0 - transmit) * source
            upward_rows.append(jnp.sum(upward, axis=0))
        return upward, jnp.stack(upward_rows[::-1])

    up_init = emission_share[:, None] * (radiant_ground ** 4)[None, :]
    final_up, up_rows = lax.scan(up_block, up_init, block_ids, reverse=True)
    upward_flux = jnp.concatenate([up_rows.reshape(strata_range, radiant_span), jnp.sum(up_init, axis=0)[None]], axis=0)
    net_flux = thermal_down - upward_flux + direct_down
    return (net_flux[:-1] - net_flux[1:]) / radiant_depth


def reference(stratum_warmth_anomaly, pressure_depth, absorber_amounts, ground_warmth_anomaly, sun_elevation_factor, daytime_mask, dispatch_position, arrival_membership, adjacency_table, blending_coefficient, opacity_table, emission_share, sunshine_share):
    overall_summation = stratum_warmth_anomaly.shape[1]
    cell_sequence = dispatch_position.shape[1]
    per_peer = cell_sequence // dispatch_position.shape[0]
    groups_dev = cell_sequence // 4
    rad_total = overall_summation // 4
    column_ids = jnp.arange(overall_summation, dtype=jnp.int32)
    source_dev = column_ids // cell_sequence
    position = dispatch_position.reshape(-1).astype(jnp.int32)
    target = position // per_peer
    received = source_dev * per_peer + position % per_peer
    rad_ids = (target * groups_dev + arrival_membership[target, received] // 4).astype(jnp.int32)

    def average_quantity(quantity):
        moved = jnp.moveaxis(quantity, -1, 0)
        summed = jax.ops.segment_sum(moved, rad_ids, num_segments=rad_total)
        return jnp.moveaxis(summed, 0, -1) * 0.25

    radiant_warmth = average_quantity(stratum_warmth_anomaly)
    radiant_depth = average_quantity(pressure_depth)
    radiant_species = average_quantity(absorber_amounts)
    radiant_ground = average_quantity(ground_warmth_anomaly)
    sunlight_incline = average_quantity(sun_elevation_factor)
    incoming_sunshine = average_quantity(daytime_mask.astype(jnp.float32) * sun_elevation_factor)
    radiant_heating = compute_flux_heating(radiant_warmth, radiant_depth, radiant_species, radiant_ground, sunlight_incline, incoming_sunshine, opacity_table, emission_share, sunshine_share)
    heating = jnp.take(radiant_heating, rad_ids, axis=1)

    base_ids = source_dev * cell_sequence - HALO
    mixed = absorber_amounts
    for step_id in range(STEPS):
        update = jnp.zeros_like(mixed)
        for near_id in range(adjacency_table.shape[0]):
            source_ids = ((base_ids + adjacency_table[near_id]) % overall_summation).astype(jnp.int32)
            update = update + blending_coefficient[near_id] * (jnp.take(mixed, source_ids, axis=2) - mixed)
        mixed = mixed + update
    return heating, mixed
```

```python
import functools

import jax
import jax.numpy as jnp
from jax import lax
from jax.experimental import pallas as pl
from jax.experimental.pallas import tpu as pltpu
from jax.sharding import PartitionSpec as P

STEPS = 4
LEVEL_BLOCK = 9
HALO = 64


DIFFUSE = 1.66
TOP = lax.Precision.HIGHEST


def padded(shard, sides, width):
    for axis, dim in sides:
        size, length = (lax.axis_size(axis), shard.shape[dim])
        up = [(i, (i + 1) % size) for i in range(size)]
        down = [(j, i) for i, j in up]
        last = lax.slice_in_dim(shard, length - width, length, axis=dim)
        first = lax.slice_in_dim(shard, 0, width, axis=dim)
        before = lax.ppermute(last, axis, up)
        after = lax.ppermute(first, axis, down)
        shard = jnp.concatenate([before, shard, after], axis=dim)
    return shard


def select_matrix(ids, count):
    return (ids[:, None] == jnp.arange(count, dtype=jnp.int32)[None, :]).astype(jnp.float32)


def pick_columns(values, selector):
    return lax.dot_general(values, selector, (((1,), (1,)), ((), ())), precision=TOP)


def optical(level_table, radiant_species, stratum_index):
    coeffs = lax.dynamic_index_in_dim(level_table, stratum_index, 0, keepdims=False)
    amounts = lax.dynamic_index_in_dim(radiant_species, stratum_index, 1, keepdims=False)
    optical_depth = coeffs[0][:, None] * amounts[0][None, :]
    for species in range(1, coeffs.shape[0]):
        optical_depth = optical_depth + coeffs[species][:, None] * amounts[species][None, :]
    return optical_depth


def compute_flux_heating(
    radiant_warmth,
    radiant_depth,
    radiant_species,
    radiant_ground,
    sunlight_incline,
    incoming_sunshine,
    opacity_table,
    emission_share,
    sunshine_share,
):
    strata_range, radiant_span = radiant_warmth.shape
    blocks = strata_range // LEVEL_BLOCK
    gpoints = emission_share.shape[0]
    block_ids = jnp.arange(blocks, dtype=jnp.int32)
    level_table = jnp.transpose(opacity_table, (2, 0, 1))

    def layer_terms(stratum_index):
        optical_depth = optical(level_table, radiant_species, stratum_index)
        stratum_warmth = lax.dynamic_index_in_dim(radiant_warmth, stratum_index, 0, keepdims=False)
        source = emission_share[:, None] * (stratum_warmth**4)[None, :]
        return (optical_depth, jnp.exp(-DIFFUSE * optical_depth), source)

    def down_block(fluxes, block_id):
        thermal, direct = fluxes
        thermal_rows = []
        direct_rows = []
        for inner_id in range(LEVEL_BLOCK):
            optical_depth, transmit, source = layer_terms(block_id * LEVEL_BLOCK + inner_id)
            thermal = transmit * thermal + (1.0 - transmit) * source
            direct = direct * jnp.exp(-optical_depth / sunlight_incline[None, :])
            thermal_rows.append(jnp.sum(thermal, axis=0))
            direct_rows.append(jnp.sum(direct, axis=0))
        return ((thermal, direct), (jnp.stack(thermal_rows), jnp.stack(direct_rows)))

    down_init = (
        jnp.zeros((gpoints, radiant_span), jnp.float32),
        sunshine_share[:, None] * incoming_sunshine[None, :],
    )
    final_down, (down_rows, direct_rows) = lax.scan(down_block, down_init, block_ids)
    thermal_down = jnp.concatenate(
        [jnp.zeros((1, radiant_span), jnp.float32), down_rows.reshape(strata_range, radiant_span)],
        axis=0,
    )
    direct_down = jnp.concatenate(
        [jnp.sum(down_init[1], axis=0)[None], direct_rows.reshape(strata_range, radiant_span)],
        axis=0,
    )

    def up_block(upward, block_id):
        upward_rows = []
        for inner_id in range(LEVEL_BLOCK - 1, -1, -1):
            optical_depth, transmit, source = layer_terms(block_id * LEVEL_BLOCK + inner_id)
            upward = transmit * upward + (1.0 - transmit) * source
            upward_rows.append(jnp.sum(upward, axis=0))
        return (upward, jnp.stack(upward_rows[::-1]))

    up_init = emission_share[:, None] * (radiant_ground**4)[None, :]
    final_up, up_rows = lax.scan(up_block, up_init, block_ids, reverse=True)
    upward_flux = jnp.concatenate(
        [up_rows.reshape(strata_range, radiant_span), jnp.sum(up_init, axis=0)[None]], axis=0
    )
    net_flux = thermal_down - upward_flux + direct_down
    return (net_flux[:-1] - net_flux[1:]) / radiant_depth


def plain_device(
    stratum_warmth_anomaly,
    pressure_depth,
    absorber_amounts,
    ground_warmth_anomaly,
    sun_elevation_factor,
    daytime_mask,
    dispatch_position,
    arrival_membership,
    adjacency_table,
    blending_coefficient,
    opacity_table,
    emission_share,
    sunshine_share,
):
    cell_sequence = stratum_warmth_anomaly.shape[1]
    position = dispatch_position[0]
    placing = select_matrix(position, cell_sequence)
    state_bundle = jnp.concatenate(
        [stratum_warmth_anomaly[None], pressure_depth[None], absorber_amounts], axis=0
    )
    surface = jnp.stack(
        [
            ground_warmth_anomaly,
            sun_elevation_factor,
            daytime_mask.astype(jnp.float32) * sun_elevation_factor,
        ],
        axis=0,
    )[:, None, :]
    packed = jnp.dot(state_bundle.reshape(-1, cell_sequence), placing, precision=TOP).reshape(
        state_bundle.shape
    )
    packed_surface = jnp.dot(surface.reshape(3, cell_sequence), placing, precision=TOP).reshape(
        surface.shape
    )
    groups_dev = cell_sequence // 4
    group_ids = arrival_membership[0] // 4
    half_arrived, arrived_surface = (
        lax.all_to_all(packed, "grp", split_axis=2, concat_axis=2, tiled=True),
        lax.all_to_all(packed_surface, "grp", split_axis=2, concat_axis=2, tiled=True),
    )
    arrived = lax.all_gather(half_arrived, "sec", axis=1, tiled=True)
    selector = select_matrix(group_ids, groups_dev)
    member = selector * 0.25
    flattened = arrived.reshape(-1, cell_sequence)
    pooled = jnp.dot(flattened, member, precision=TOP).reshape(
        arrived.shape[0], arrived.shape[1], groups_dev
    )
    pooled_surface = jnp.dot(arrived_surface.reshape(3, cell_sequence), member, precision=TOP)
    heat_part = compute_flux_heating(
        pooled[0],
        pooled[1],
        pooled[2:],
        pooled_surface[0],
        pooled_surface[1],
        pooled_surface[2],
        opacity_table,
        emission_share,
        sunshine_share,
    )
    slot_heat = pick_columns(heat_part, selector)
    returned = lax.all_to_all(slot_heat, "grp", split_axis=1, concat_axis=1, tiled=True)
    own_heat = pick_columns(returned, placing)
    heating = lax.psum_scatter(own_heat, "sec", scatter_dimension=0, tiled=True)
    extended_span = cell_sequence + 2 * HALO
    source_rows = jnp.arange(extended_span, dtype=jnp.int32)[:, None]
    blend_matrix = jnp.zeros((extended_span, cell_sequence), jnp.float32)
    for near_id in range(adjacency_table.shape[0]):
        blend_matrix = blend_matrix + jnp.where(
            adjacency_table[near_id][None, :] == source_rows,
            blending_coefficient[near_id][None, :],
            0.0,
        )
    centre_rows = jnp.arange(cell_sequence, dtype=jnp.int32)[None, :] + HALO
    weight_total = jnp.sum(blending_coefficient, axis=0)
    blend_matrix = blend_matrix - jnp.where(source_rows == centre_rows, weight_total[None, :], 0.0)
    mixed = absorber_amounts
    for step_id in range(STEPS):
        extended = padded(mixed, (("grp", 2),), HALO)
        update = jnp.dot(extended.reshape(-1, extended_span), blend_matrix, precision=TOP).reshape(
            mixed.shape
        )
        mixed = mixed + update
    return (heating, mixed)


LANES = 128
NT = (((1,), (1,)), ((), ()))
VMEM = pl.BlockSpec(memory_space=pltpu.VMEM)
MESH = pl.DeviceIdType.MESH


def halves(value):
    high = value.astype(jnp.bfloat16)
    low = (value - high.astype(jnp.float32)).astype(jnp.bfloat16)
    return high, low


def iota(shape, dim):
    return lax.broadcasted_iota(jnp.int32, shape, dim)


def one_hot(cond):
    return jnp.where(cond, 1.0, 0.0).astype(jnp.bfloat16)


def mm(left, right, dims=(((1,), (0,)), ((), ()))):
    return lax.dot_general(left, right, dims, preferred_element_type=jnp.float32)


def greet(n):
    me, side = lax.axis_index("grp"), lax.axis_index("sec")
    barrier = pltpu.get_barrier_semaphore()
    for d in range(1, n):
        peer = lax.rem(me + d, n)
        pl.semaphore_signal(barrier, inc=1, device_id={"grp": peer}, device_id_type=MESH)
    pl.semaphore_signal(barrier, inc=1, device_id={"sec": 1 - side}, device_id_type=MESH)
    pl.semaphore_wait(barrier, n)
    return me, side


def remote(src, dst, send_sem, recv_sem, device):
    return pltpu.make_async_remote_copy(
        src_ref=src, dst_ref=dst, send_sem=send_sem, recv_sem=recv_sem,
        device_id=device, device_id_type=MESH,
    )


def dispatch_kernel(
    n, temp, depth, absorb, ground, sun, mask, pos, memb, adj, blend,
    mixed_out, pooled_out,
    data, send, recv, halo_l, halo_r, adj_l, adj_r, blend_l, blend_r,
    grid_a, grid_b, mix_hi, mix_lo, pooled,
    out_sem, in_sem, hs_sem, hr_sem, ps_sem, pr_sem,
):
    species, levels, cols = absorb.shape
    rows = -(-(levels + 3) // 8) * 8
    per = cols // n
    pack = per // 4
    rads = cols // 4
    wide = STEPS * HALO
    me, side = greet(n)
    right, left = lax.rem(me + 1, n), lax.rem(me + n - 1, n)

    halo = []
    for k, (src, to_left, to_right) in enumerate(
        ((absorb, halo_r, halo_l), (adj, adj_r, adj_l), (blend, blend_r, blend_l))
    ):
        lead = (slice(None),) * (len(src.shape) - 1)
        first, last = src.at[lead + (pl.ds(0, wide),)], src.at[lead + (pl.ds(cols - wide, wide),)]
        halo.append(remote(first, to_left, hs_sem.at[2 * k], hr_sem.at[2 * k], {"grp": left}))
        halo.append(remote(last, to_right, hs_sem.at[2 * k + 1], hr_sem.at[2 * k + 1], {"grp": right}))
    for copy in halo:
        copy.start()

    data[...] = jnp.zeros_like(data)
    data[0:levels, :] = temp[...]
    data[rows : rows + levels, :] = depth[...]
    for s in range(species):
        data[(2 + s) * rows : (2 + s) * rows + levels, :] = absorb[s]
    data[levels : levels + 1, :] = ground[...]
    data[levels + 1 : levels + 2, :] = sun[...]
    data[levels + 2 : levels + 3, :] = mask[...].astype(jnp.float32) * sun[...]
    rest = data[2 * LANES : 2 * LANES + 32, :]
    for q in range(1, 4):
        data[2 * LANES + 32 * q : 2 * LANES + 32 * (q + 1), :] = rest
    data_hi, data_lo = halves(data[...])
    relative = pos[...] - me * per
    relative = jnp.where(relative < 0, relative + cols, relative)
    chunk = 4 * per
    lane_block = iota((4, pack, LANES), 2) // 32
    copies = []
    for c in range(n // 4):
        hot = one_hot(iota((chunk, cols), 0) + c * chunk == relative)
        out = mm(hot, data_hi, NT) + mm(hot, data_lo, NT)
        send[4 * c : 4 * c + 4, 0:per, :] = out[:, 0:LANES].reshape(4, per, LANES)
        send[4 * c : 4 * c + 4, per : 2 * per, :] = out[:, LANES : 2 * LANES].reshape(4, per, LANES)
        tail = out[:, 2 * LANES :].reshape(4, 4, pack, LANES)
        folded = jnp.where(lane_block == 0, tail[:, 0], 0.0)
        for q in range(1, 4):
            folded = jnp.where(lane_block == q, tail[:, q], folded)
        send[4 * c : 4 * c + 4, 2 * per :, :] = folded
        for d in range(max(4 * c, 1), 4 * c + 4):
            copy = remote(
                send.at[d], recv.at[me], out_sem.at[d], in_sem.at[d], {"grp": lax.rem(me + d, n)}
            )
            copy.start()
            copies.append(copy)
    recv[me] = send[0]

    grid_a[...] = jnp.zeros_like(grid_a)
    grid_b[...] = jnp.zeros_like(grid_b)
    for s in range(species):
        grid_a[s * rows : s * rows + levels, wide : wide + cols] = absorb[s]
    for copy in halo:
        copy.wait()
    for s in range(species):
        grid_a[s * rows : s * rows + levels, 0:wide] = halo_l[s]
        grid_a[s * rows : s * rows + levels, wide + cols :] = halo_r[s]
    span = cols + 2 * wide
    tables = (
        (adj_l[...] - HALO + wide - cols, blend_l[...]),
        (adj[...] - HALO + wide, blend[...]),
        (adj_r[...] - HALO + wide + cols, blend_r[...]),
    )
    table = jnp.concatenate([t[0] for t in tables], axis=1)
    weight = jnp.concatenate([t[1] for t in tables], axis=1)
    total = jnp.sum(weight, axis=0, keepdims=True)
    width = 256
    windows = []
    for b in range(span // width):
        low, high = max(0, width * b - LANES), min(span, width * (b + 1) + LANES)
        windows.append((low, high))
        source = iota((high - low, width), 0) + low
        matrix = jnp.zeros((high - low, width), jnp.float32)
        here = slice(width * b, width * (b + 1))
        for k in range(table.shape[0]):
            matrix = matrix + jnp.where(table[k : k + 1, here] == source, weight[k : k + 1, here], 0.0)
        hi, lo = halves(matrix)
        mix_hi[b, 0 : high - low, :] = hi
        mix_lo[b, 0 : high - low, :] = lo
    old, new = grid_a, grid_b
    for step in range(STEPS):
        blocks = range(span // width)
        if step == STEPS - 1:
            blocks = range(wide // width, (wide + cols) // width)
        for b in blocks:
            low, high = windows[b]
            here = slice(width * b, width * (b + 1))
            hi, lo = halves(old[:, low:high])
            left_hi = mix_hi[b, 0 : high - low, :]
            update = mm(hi, left_hi) + mm(lo, left_hi) + mm(hi, mix_lo[b, 0 : high - low, :])
            centre = old[:, here]
            new[:, here] = centre + (update - total[:, here] * centre)
        old, new = new, old
    for s in range(species):
        mixed_out[s] = old[s * rows : s * rows + levels, wide : wide + cols]

    member = one_hot(iota((rads, cols), 0) == lax.shift_right_logical(memb[...], 2))
    for copy in copies:
        copy.wait()
    whole = recv[...]
    parts = [whole[:, 0:per, :].reshape(cols, LANES), whole[:, per : 2 * per, :].reshape(cols, LANES)]
    tail = whole[:, 2 * per :, :]
    big_block = iota((n, pack, LANES), 2) // 32
    tail = jnp.stack([jnp.where(big_block == q, tail, 0.0) for q in range(4)], axis=1)
    parts.append(tail.reshape(cols, LANES))
    for k, part in enumerate(parts):
        hi, lo = halves(part)
        pooled[side, k] = (mm(member, hi) + mm(member, lo)) * 0.25
    copy = remote(pooled.at[side], pooled.at[side], ps_sem, pr_sem, {"sec": 1 - side})
    copy.start()
    copy.wait()
    pooled_out[...] = pooled[...]


def dispatch(n, *args):
    absorb = args[2]
    species, levels, cols = absorb.shape
    rows = -(-(levels + 3) // 8) * 8
    per = cols // n
    slab = 2 * per + per // 4
    wide = STEPS * HALO
    near = args[8].shape[0]
    span = cols + 2 * wide
    dma = pltpu.SemaphoreType.DMA
    f32 = jnp.float32
    return pl.pallas_call(
        functools.partial(dispatch_kernel, n),
        out_shape=(
            jax.ShapeDtypeStruct(absorb.shape, f32),
            jax.ShapeDtypeStruct((2, 3, cols // 4, LANES), f32),
        ),
        in_specs=[VMEM] * len(args),
        out_specs=(VMEM, VMEM),
        scratch_shapes=[
            pltpu.VMEM((3 * LANES, cols), f32),
            pltpu.VMEM((n, slab, LANES), f32),
            pltpu.VMEM((n, slab, LANES), f32),
            pltpu.VMEM((species, levels, wide), f32),
            pltpu.VMEM((species, levels, wide), f32),
            pltpu.VMEM((near, wide), jnp.int32),
            pltpu.VMEM((near, wide), jnp.int32),
            pltpu.VMEM((near, wide), f32),
            pltpu.VMEM((near, wide), f32),
            pltpu.VMEM((species * rows, span), f32),
            pltpu.VMEM((species * rows, span), f32),
            pltpu.VMEM((span // 256, 512, 256), jnp.bfloat16),
            pltpu.VMEM((span // 256, 512, 256), jnp.bfloat16),
            pltpu.VMEM((2, 3, cols // 4, LANES), f32),
            dma((n,)), dma((n,)), dma((6,)), dma((6,)), dma, dma,
        ],
        compiler_params=pltpu.CompilerParams(
            collective_id=0, has_side_effects=True, vmem_limit_bytes=40 << 20
        ),
        cost_estimate=pl.CostEstimate(flops=10**9, bytes_accessed=4 << 20, transcendentals=0),
    )(*args)


def sweep_kernel(n, levels, pooled, memb, opacity, emission, sunshine, slots_out, state, trans, net):
    rows = -(-(levels + 3) // 8) * 8
    gpoints = emission.shape[0]
    strata = opacity.shape[2]
    rads = pooled.shape[2]
    cols = memb.shape[1]
    for h in range(2):
        state[h, 0:LANES, :] = pooled[h, 0].T
        state[h, LANES : 2 * LANES, :] = pooled[h, 1].T
        tail = pooled[h, 2].T
        state[h, 2 * LANES :, :] = tail[0:32] + tail[32:64] + tail[64:96] + tail[96:128]

    def row(field, level):
        at = field * rows + level % levels
        return state[level // levels, at : at + 1, :]

    ground = state[0, levels : levels + 1, :]
    incline = state[0, levels + 1 : levels + 2, :]
    incoming = state[0, levels + 2 : levels + 3, :]
    share = jnp.broadcast_to(emission[...], (gpoints, rads))
    slant = -1.0 / incline

    def gsum(value):
        return jnp.sum(value.reshape(gpoints // 8, 8, rads), axis=0)

    def fourth(value):
        square = value * value
        return square * square

    thermal = jnp.zeros((gpoints, rads), jnp.float32)
    direct = sunshine[...] * incoming
    net[0] = gsum(direct)
    for level in range(strata):
        tau = opacity[0, :, level : level + 1] * row(2, level)
        for s in range(1, opacity.shape[0]):
            tau = tau + opacity[s, :, level : level + 1] * row(2 + s, level)
        transmit = jnp.exp(-DIFFUSE * tau)
        trans[level] = transmit
        source = share * fourth(row(0, level))
        thermal = source + transmit * (thermal - source)
        direct = direct * jnp.exp(tau * slant)
        net[level + 1] = gsum(thermal + direct)
    upward = share * fourth(ground)
    net[strata] = net[strata] - gsum(upward)
    for level in range(strata - 1, -1, -1):
        source = share * fourth(row(0, level))
        upward = source + trans[level] * (upward - source)
        net[level] = net[level] - gsum(upward)

    member = one_hot(iota((rads, cols), 0) == lax.shift_right_logical(memb[...], 2))
    per = cols // n
    fold = per // 2
    half_lane = iota((n, fold, LANES), 2) // 64
    fill = jnp.zeros((64 - levels, rads), jnp.float32)
    for h in range(2):
        change = net[h * levels : (h + 1) * levels] - net[h * levels + 1 : (h + 1) * levels + 1]
        heat = jnp.sum(change, axis=1) / state[h, rows : rows + levels, :]
        heat = jnp.concatenate([heat, fill], axis=0)
        hi, lo = halves(jnp.concatenate([heat, heat], axis=0))
        spread = (mm(hi, member) + mm(lo, member)).T.reshape(n, 2, fold, LANES)
        slots_out[h] = jnp.where(half_lane == 0, spread[:, 0], spread[:, 1])


def sweep(n, levels, pooled, memb, opacity, emission, sunshine):
    rows = -(-(levels + 3) // 8) * 8
    gpoints = emission.shape[0]
    strata = opacity.shape[2]
    rads = pooled.shape[2]
    per = memb.shape[1] // n
    f32 = jnp.float32
    return pl.pallas_call(
        functools.partial(sweep_kernel, n, levels),
        out_shape=jax.ShapeDtypeStruct((2, n, per // 2, LANES), f32),
        in_specs=[VMEM] * 5,
        out_specs=VMEM,
        scratch_shapes=[
            pltpu.VMEM((2, 6 * rows, rads), f32),
            pltpu.VMEM((strata, gpoints, rads), f32),
            pltpu.VMEM((strata + 1, 8, rads), f32),
        ],
        compiler_params=pltpu.CompilerParams(vmem_limit_bytes=40 << 20),
        cost_estimate=pl.CostEstimate(flops=2 * 10**7, bytes_accessed=1 << 20, transcendentals=10**6),
    )(pooled, memb, opacity, emission, sunshine)


def return_kernel(n, slots, out, other, send, recv, s_sem, r_sem, out_sem, in_sem):
    me, side = greet(n)
    copy = remote(slots.at[1 - side], other, s_sem, r_sem, {"sec": 1 - side})
    copy.start()
    copy.wait()
    send[...] = slots[side] + other[...]
    copies = []
    for d in range(1, n):
        peer = lax.rem(me + d, n)
        copy = remote(send.at[peer], recv.at[me], out_sem.at[d], in_sem.at[d], {"grp": peer})
        copy.start()
        copies.append(copy)
    recv[me] = send[me]
    for copy in copies:
        copy.wait()
    out[...] = recv[...]


def give_back(n, slots):
    shape = slots.shape[1:]
    f32 = jnp.float32
    dma = pltpu.SemaphoreType.DMA
    return pl.pallas_call(
        functools.partial(return_kernel, n),
        out_shape=jax.ShapeDtypeStruct(shape, f32),
        in_specs=[VMEM],
        out_specs=VMEM,
        scratch_shapes=[
            pltpu.VMEM(shape, f32), pltpu.VMEM(shape, f32), pltpu.VMEM(shape, f32),
            dma, dma, dma((n,)), dma((n,)),
        ],
        compiler_params=pltpu.CompilerParams(collective_id=1, has_side_effects=True),
        cost_estimate=pl.CostEstimate(flops=10**5, bytes_accessed=1 << 20, transcendentals=0),
    )(slots)


def unpack_kernel(n, returned, pos, heating):
    levels, cols = heating.shape
    fold = returned.shape[1]
    value = returned[...].reshape(n * fold, LANES).T
    place = iota((n * fold, cols), 0)
    place = (place // fold) * (2 * fold) + lax.rem(place, fold)
    total = None
    for q in range(2):
        hot = one_hot(place + q * fold == pos[...])
        hi, lo = halves(value[64 * q : 64 * (q + 1)])
        part = mm(hi, hot) + mm(lo, hot)
        total = part if total is None else total + part
    heating[...] = total[0:levels]


def unpack(n, levels, returned, pos):
    return pl.pallas_call(
        functools.partial(unpack_kernel, n),
        out_shape=jax.ShapeDtypeStruct((levels, pos.shape[1]), jnp.float32),
        in_specs=[VMEM] * 2,
        out_specs=VMEM,
        compiler_params=pltpu.CompilerParams(vmem_limit_bytes=32 << 20),
        cost_estimate=pl.CostEstimate(flops=10**8, bytes_accessed=1 << 20, transcendentals=0),
    )(returned, pos)


def folds_evenly(n, sides, levels, cols, species, gpoints):
    rows = -(-(levels + 3) // 8) * 8
    return (
        n > 3 and n % 4 == 0 and sides == 2 and species == 4
        and cols == n * 32 and cols == 4 * LANES and 2 * STEPS * HALO == cols
        and 6 * rows == 2 * LANES + 32 and gpoints % 8 == 0
    )


def per_device(*args):
    (warmth, depth, absorb, ground, sun, mask, pos, memb, adj, blend, opacity, emission, sunshine) = args
    n = lax.axis_size("grp")
    levels, cols = warmth.shape
    gpoints = emission.shape[0]
    if not folds_evenly(n, lax.axis_size("sec"), levels, cols, absorb.shape[0], gpoints):
        return plain_device(*args)
    mixed, pooled = dispatch(
        n, warmth, depth, absorb, ground[None], sun[None], mask[None], pos, memb, adj, blend
    )
    slots = sweep(n, levels, pooled, memb, opacity, emission[:, None], sunshine[:, None])
    returned = give_back(n, slots)
    return (unpack(n, levels, returned, pos), mixed)


def solution(mesh):
    in_specs = (
        P("sec", "grp"),
        P("sec", "grp"),
        P(None, "sec", "grp"),
        P("grp"),
        P("grp"),
        P("grp"),
        P("grp", None),
        P("grp", None),
        P(None, "grp"),
        P(None, "grp"),
        P(None, "sec", None),
        P("sec"),
        P("sec"),
    )
    out_specs = (P("sec", "grp"), P(None, "sec", "grp"))
    return jax.shard_map(
        per_device, mesh=mesh, in_specs=in_specs, out_specs=out_specs, check_vma=False
    )
```

```python
import functools

import jax
import jax.numpy as jnp
from jax import lax
from jax.experimental import pallas as pl
from jax.experimental.pallas import tpu as pltpu
from jax.sharding import PartitionSpec as P

STEPS = 4
LEVEL_BLOCK = 9
HALO = 64


DIFFUSE = 1.66
TOP = lax.Precision.HIGHEST


def padded(shard, sides, width):
    for axis, dim in sides:
        size, length = (lax.axis_size(axis), shard.shape[dim])
        up = [(i, (i + 1) % size) for i in range(size)]
        down = [(j, i) for i, j in up]
        last = lax.slice_in_dim(shard, length - width, length, axis=dim)
        first = lax.slice_in_dim(shard, 0, width, axis=dim)
        before = lax.ppermute(last, axis, up)
        after = lax.ppermute(first, axis, down)
        shard = jnp.concatenate([before, shard, after], axis=dim)
    return shard


def select_matrix(ids, count):
    return (ids[:, None] == jnp.arange(count, dtype=jnp.int32)[None, :]).astype(jnp.float32)


def pick_columns(values, selector):
    return lax.dot_general(values, selector, (((1,), (1,)), ((), ())), precision=TOP)


def optical(level_table, radiant_species, stratum_index):
    coeffs = lax.dynamic_index_in_dim(level_table, stratum_index, 0, keepdims=False)
    amounts = lax.dynamic_index_in_dim(radiant_species, stratum_index, 1, keepdims=False)
    optical_depth = coeffs[0][:, None] * amounts[0][None, :]
    for species in range(1, coeffs.shape[0]):
        optical_depth = optical_depth + coeffs[species][:, None] * amounts[species][None, :]
    return optical_depth


def compute_flux_heating(
    radiant_warmth,
    radiant_depth,
    radiant_species,
    radiant_ground,
    sunlight_incline,
    incoming_sunshine,
    opacity_table,
    emission_share,
    sunshine_share,
):
    strata_range, radiant_span = radiant_warmth.shape
    blocks = strata_range // LEVEL_BLOCK
    gpoints = emission_share.shape[0]
    block_ids = jnp.arange(blocks, dtype=jnp.int32)
    level_table = jnp.transpose(opacity_table, (2, 0, 1))

    def layer_terms(stratum_index):
        optical_depth = optical(level_table, radiant_species, stratum_index)
        stratum_warmth = lax.dynamic_index_in_dim(radiant_warmth, stratum_index, 0, keepdims=False)
        source = emission_share[:, None] * (stratum_warmth**4)[None, :]
        return (optical_depth, jnp.exp(-DIFFUSE * optical_depth), source)

    def down_block(fluxes, block_id):
        thermal, direct = fluxes
        thermal_rows = []
        direct_rows = []
        for inner_id in range(LEVEL_BLOCK):
            optical_depth, transmit, source = layer_terms(block_id * LEVEL_BLOCK + inner_id)
            thermal = transmit * thermal + (1.0 - transmit) * source
            direct = direct * jnp.exp(-optical_depth / sunlight_incline[None, :])
            thermal_rows.append(jnp.sum(thermal, axis=0))
            direct_rows.append(jnp.sum(direct, axis=0))
        return ((thermal, direct), (jnp.stack(thermal_rows), jnp.stack(direct_rows)))

    down_init = (
        jnp.zeros((gpoints, radiant_span), jnp.float32),
        sunshine_share[:, None] * incoming_sunshine[None, :],
    )
    final_down, (down_rows, direct_rows) = lax.scan(down_block, down_init, block_ids)
    thermal_down = jnp.concatenate(
        [jnp.zeros((1, radiant_span), jnp.float32), down_rows.reshape(strata_range, radiant_span)],
        axis=0,
    )
    direct_down = jnp.concatenate(
        [jnp.sum(down_init[1], axis=0)[None], direct_rows.reshape(strata_range, radiant_span)],
        axis=0,
    )

    def up_block(upward, block_id):
        upward_rows = []
        for inner_id in range(LEVEL_BLOCK - 1, -1, -1):
            optical_depth, transmit, source = layer_terms(block_id * LEVEL_BLOCK + inner_id)
            upward = transmit * upward + (1.0 - transmit) * source
            upward_rows.append(jnp.sum(upward, axis=0))
        return (upward, jnp.stack(upward_rows[::-1]))

    up_init = emission_share[:, None] * (radiant_ground**4)[None, :]
    final_up, up_rows = lax.scan(up_block, up_init, block_ids, reverse=True)
    upward_flux = jnp.concatenate(
        [up_rows.reshape(strata_range, radiant_span), jnp.sum(up_init, axis=0)[None]], axis=0
    )
    net_flux = thermal_down - upward_flux + direct_down
    return (net_flux[:-1] - net_flux[1:]) / radiant_depth


def plain_device(
    stratum_warmth_anomaly,
    pressure_depth,
    absorber_amounts,
    ground_warmth_anomaly,
    sun_elevation_factor,
    daytime_mask,
    dispatch_position,
    arrival_membership,
    adjacency_table,
    blending_coefficient,
    opacity_table,
    emission_share,
    sunshine_share,
):
    cell_sequence = stratum_warmth_anomaly.shape[1]
    position = dispatch_position[0]
    placing = select_matrix(position, cell_sequence)
    state_bundle = jnp.concatenate(
        [stratum_warmth_anomaly[None], pressure_depth[None], absorber_amounts], axis=0
    )
    surface = jnp.stack(
        [
            ground_warmth_anomaly,
            sun_elevation_factor,
            daytime_mask.astype(jnp.float32) * sun_elevation_factor,
        ],
        axis=0,
    )[:, None, :]
    packed = jnp.dot(state_bundle.reshape(-1, cell_sequence), placing, precision=TOP).reshape(
        state_bundle.shape
    )
    packed_surface = jnp.dot(surface.reshape(3, cell_sequence), placing, precision=TOP).reshape(
        surface.shape
    )
    groups_dev = cell_sequence // 4
    group_ids = arrival_membership[0] // 4
    half_arrived, arrived_surface = (
        lax.all_to_all(packed, "grp", split_axis=2, concat_axis=2, tiled=True),
        lax.all_to_all(packed_surface, "grp", split_axis=2, concat_axis=2, tiled=True),
    )
    arrived = lax.all_gather(half_arrived, "sec", axis=1, tiled=True)
    selector = select_matrix(group_ids, groups_dev)
    member = selector * 0.25
    flattened = arrived.reshape(-1, cell_sequence)
    pooled = jnp.dot(flattened, member, precision=TOP).reshape(
        arrived.shape[0], arrived.shape[1], groups_dev
    )
    pooled_surface = jnp.dot(arrived_surface.reshape(3, cell_sequence), member, precision=TOP)
    heat_part = compute_flux_heating(
        pooled[0],
        pooled[1],
        pooled[2:],
        pooled_surface[0],
        pooled_surface[1],
        pooled_surface[2],
        opacity_table,
        emission_share,
        sunshine_share,
    )
    slot_heat = pick_columns(heat_part, selector)
    returned = lax.all_to_all(slot_heat, "grp", split_axis=1, concat_axis=1, tiled=True)
    own_heat = pick_columns(returned, placing)
    heating = lax.psum_scatter(own_heat, "sec", scatter_dimension=0, tiled=True)
    extended_span = cell_sequence + 2 * HALO
    source_rows = jnp.arange(extended_span, dtype=jnp.int32)[:, None]
    blend_matrix = jnp.zeros((extended_span, cell_sequence), jnp.float32)
    for near_id in range(adjacency_table.shape[0]):
        blend_matrix = blend_matrix + jnp.where(
            adjacency_table[near_id][None, :] == source_rows,
            blending_coefficient[near_id][None, :],
            0.0,
        )
    centre_rows = jnp.arange(cell_sequence, dtype=jnp.int32)[None, :] + HALO
    weight_total = jnp.sum(blending_coefficient, axis=0)
    blend_matrix = blend_matrix - jnp.where(source_rows == centre_rows, weight_total[None, :], 0.0)
    mixed = absorber_amounts
    for step_id in range(STEPS):
        extended = padded(mixed, (("grp", 2),), HALO)
        update = jnp.dot(extended.reshape(-1, extended_span), blend_matrix, precision=TOP).reshape(
            mixed.shape
        )
        mixed = mixed + update
    return (heating, mixed)


LANES = 128
NT = (((1,), (1,)), ((), ()))
VMEM = pl.BlockSpec(memory_space=pltpu.VMEM)
MESH = pl.DeviceIdType.MESH


def halves(value):
    high = value.astype(jnp.bfloat16)
    low = (value - high.astype(jnp.float32)).astype(jnp.bfloat16)
    return high, low


def iota(shape, dim):
    return lax.broadcasted_iota(jnp.int32, shape, dim)


def one_hot(cond):
    return jnp.where(cond, 1.0, 0.0).astype(jnp.bfloat16)


def mm(left, right, dims=(((1,), (0,)), ((), ()))):
    return lax.dot_general(left, right, dims, preferred_element_type=jnp.float32)


def greet(n):
    me, side = lax.axis_index("grp"), lax.axis_index("sec")
    barrier = pltpu.get_barrier_semaphore()
    for d in range(1, n):
        peer = lax.rem(me + d, n)
        pl.semaphore_signal(barrier, inc=1, device_id={"grp": peer}, device_id_type=MESH)
    pl.semaphore_signal(barrier, inc=1, device_id={"sec": 1 - side}, device_id_type=MESH)
    pl.semaphore_wait(barrier, n)
    return me, side


def remote(src, dst, send_sem, recv_sem, device):
    return pltpu.make_async_remote_copy(
        src_ref=src, dst_ref=dst, send_sem=send_sem, recv_sem=recv_sem,
        device_id=device, device_id_type=MESH,
    )


def device_kernel(
    n, temp, depth, absorb, ground, sun, mask, pos, memb, adj, blend,
    opacity, emission, sunshine, heating, mixed_out,
    data, send, recv, halo_l, halo_r, adj_l, adj_r, blend_l, blend_r,
    grid_a, grid_b, mix_hi, mix_lo, pooled,
    state, opac, trans, net, heat, other, back, home,
    out_sem, in_sem, hs_sem, hr_sem, ps_sem, pr_sem, ts_sem, tr_sem, bo_sem, bi_sem,
):
    species, levels, cols = absorb.shape
    rows = -(-(levels + 3) // 8) * 8
    per = cols // n
    pack = per // 4
    rads = cols // 4
    wide = STEPS * HALO
    me, side = greet(n)
    right, left = lax.rem(me + 1, n), lax.rem(me + n - 1, n)

    halo = []
    for k, (src, to_left, to_right) in enumerate(
        ((absorb, halo_r, halo_l), (adj, adj_r, adj_l), (blend, blend_r, blend_l))
    ):
        lead = (slice(None),) * (len(src.shape) - 1)
        first, last = src.at[lead + (pl.ds(0, wide),)], src.at[lead + (pl.ds(cols - wide, wide),)]
        halo.append(remote(first, to_left, hs_sem.at[2 * k], hr_sem.at[2 * k], {"grp": left}))
        halo.append(remote(last, to_right, hs_sem.at[2 * k + 1], hr_sem.at[2 * k + 1], {"grp": right}))
    for copy in halo:
        copy.start()

    data[...] = jnp.zeros_like(data)
    data[0:levels, :] = temp[...]
    data[rows : rows + levels, :] = depth[...]
    for s in range(species):
        data[(2 + s) * rows : (2 + s) * rows + levels, :] = absorb[s]
    data[levels : levels + 1, :] = ground[...]
    data[levels + 1 : levels + 2, :] = sun[...]
    data[levels + 2 : levels + 3, :] = mask[...].astype(jnp.float32) * sun[...]
    rest = data[2 * LANES : 2 * LANES + 32, :]
    for q in range(1, 4):
        data[2 * LANES + 32 * q : 2 * LANES + 32 * (q + 1), :] = rest
    data_hi, data_lo = halves(data[...])
    relative = pos[...] - me * per
    relative = jnp.where(relative < 0, relative + cols, relative)
    chunk = 4 * per
    lane_block = iota((4, pack, LANES), 2) // 32
    copies = []
    for c in range(n // 4):
        hot = one_hot(iota((chunk, cols), 0) + c * chunk == relative)
        out = mm(hot, data_hi, NT) + mm(hot, data_lo, NT)
        send[4 * c : 4 * c + 4, 0:per, :] = out[:, 0:LANES].reshape(4, per, LANES)
        send[4 * c : 4 * c + 4, per : 2 * per, :] = out[:, LANES : 2 * LANES].reshape(4, per, LANES)
        tail = out[:, 2 * LANES :].reshape(4, 4, pack, LANES)
        folded = jnp.where(lane_block == 0, tail[:, 0], 0.0)
        for q in range(1, 4):
            folded = jnp.where(lane_block == q, tail[:, q], folded)
        send[4 * c : 4 * c + 4, 2 * per :, :] = folded
        for d in range(max(4 * c, 1), 4 * c + 4):
            copy = remote(
                send.at[d], recv.at[me], out_sem.at[d], in_sem.at[d], {"grp": lax.rem(me + d, n)}
            )
            copy.start()
            copies.append(copy)
    recv[me] = send[0]

    grid_a[...] = jnp.zeros_like(grid_a)
    grid_b[...] = jnp.zeros_like(grid_b)
    for s in range(species):
        grid_a[s * rows : s * rows + levels, wide : wide + cols] = absorb[s]
    for copy in halo:
        copy.wait()
    for s in range(species):
        grid_a[s * rows : s * rows + levels, 0:wide] = halo_l[s]
        grid_a[s * rows : s * rows + levels, wide + cols :] = halo_r[s]
    span = cols + 2 * wide
    tables = (
        (adj_l[...] - HALO + wide - cols, blend_l[...]),
        (adj[...] - HALO + wide, blend[...]),
        (adj_r[...] - HALO + wide + cols, blend_r[...]),
    )
    table = jnp.concatenate([t[0] for t in tables], axis=1)
    weight = jnp.concatenate([t[1] for t in tables], axis=1)
    total = jnp.sum(weight, axis=0, keepdims=True)
    width = 256
    windows = []
    for b in range(span // width):
        low, high = max(0, width * b - LANES), min(span, width * (b + 1) + LANES)
        windows.append((low, high))
        source = iota((high - low, width), 0) + low
        matrix = jnp.zeros((high - low, width), jnp.float32)
        here = slice(width * b, width * (b + 1))
        for k in range(table.shape[0]):
            matrix = matrix + jnp.where(table[k : k + 1, here] == source, weight[k : k + 1, here], 0.0)
        hi, lo = halves(matrix)
        mix_hi[b, 0 : high - low, :] = hi
        mix_lo[b, 0 : high - low, :] = lo
    old, new = grid_a, grid_b
    for step in range(STEPS):
        blocks = range(span // width)
        if step == STEPS - 1:
            blocks = range(wide // width, (wide + cols) // width)
        for b in blocks:
            low, high = windows[b]
            here = slice(width * b, width * (b + 1))
            hi, lo = halves(old[:, low:high])
            left_hi = mix_hi[b, 0 : high - low, :]
            update = mm(hi, left_hi) + mm(lo, left_hi) + mm(hi, mix_lo[b, 0 : high - low, :])
            centre = old[:, here]
            new[:, here] = centre + (update - total[:, here] * centre)
        old, new = new, old
    for s in range(species):
        mixed_out[s] = old[s * rows : s * rows + levels, wide : wide + cols]

    gpoints = emission.shape[1]
    strata = opacity.shape[2]
    for b in range(strata // LEVEL_BLOCK):
        for k in range(species):
            opac[b, k * gpoints : (k + 1) * gpoints, 0:LEVEL_BLOCK] = opacity[
                k, :, b * LEVEL_BLOCK : (b + 1) * LEVEL_BLOCK
            ]
    diagonal = iota((gpoints, gpoints), 0) == iota((gpoints, gpoints), 1)
    share = jnp.sum(jnp.where(diagonal, emission[...], 0.0), axis=1, keepdims=True)
    sunny = jnp.sum(jnp.where(diagonal, sunshine[...], 0.0), axis=1, keepdims=True)
    share = jnp.broadcast_to(share, (gpoints, rads))
    member = one_hot(iota((rads, cols), 0) == lax.shift_right_logical(memb[...], 2))

    for copy in copies:
        copy.wait()
    whole = recv[...]
    parts = [whole[:, 0:per, :].reshape(cols, LANES), whole[:, per : 2 * per, :].reshape(cols, LANES)]
    tail = whole[:, 2 * per :, :]
    big_block = iota((n, pack, LANES), 2) // 32
    tail = jnp.stack([jnp.where(big_block == q, tail, 0.0) for q in range(4)], axis=1)
    parts.append(tail.reshape(cols, LANES))
    for k, part in enumerate(parts):
        hi, lo = halves(part)
        pooled[side, k] = (mm(member, hi) + mm(member, lo)) * 0.25
    copy = remote(pooled.at[side], pooled.at[side], ps_sem, pr_sem, {"sec": 1 - side})
    copy.start()
    copy.wait()

    for h in range(2):
        tail = pooled[h, 2].T
        tail = tail[0:32] + tail[32:64] + tail[64:96] + tail[96:128]
        field = jnp.concatenate([pooled[h, 0].T, pooled[h, 1].T, tail], axis=0)
        for k in range(2 + species):
            state[k, h * levels : (h + 1) * levels, :] = field[k * rows : k * rows + levels]
        surface = field[levels : levels + 3]

    def fourth(value):
        square = value * value
        return square * square

    def gsum(value):
        return jnp.sum(value.reshape(gpoints // 8, 8, rads), axis=0)

    slant = -1.0 / surface[1:2]
    state[0, 0:strata, :] = fourth(state[0, 0:strata, :])

    def down(b, fluxes):
        thermal, direct = fluxes
        coeffs = opac[b]
        for i in range(LEVEL_BLOCK):
            level = b * LEVEL_BLOCK + i
            tau = None
            for k in range(species):
                part = coeffs[k * gpoints : (k + 1) * gpoints, i : i + 1] * state[2 + k, pl.ds(level, 1), :]
                tau = part if tau is None else tau + part
            transmit = jnp.exp(-DIFFUSE * tau)
            trans[level] = transmit
            source = share * state[0, pl.ds(level, 1), :]
            thermal = source + transmit * (thermal - source)
            direct = direct * jnp.exp(tau * slant)
            net[level + 1] = gsum(thermal + direct)
        return thermal, direct

    direct = sunny * surface[2:3]
    net[0] = gsum(direct)
    lax.fori_loop(0, strata // LEVEL_BLOCK, down, (jnp.zeros((gpoints, rads), jnp.float32), direct))
    upward = share * fourth(surface[0:1])
    net[strata] = net[strata] - gsum(upward)

    def up(b, upward):
        for i in range(LEVEL_BLOCK):
            level = strata - 1 - (b * LEVEL_BLOCK + i)
            source = share * state[0, pl.ds(level, 1), :]
            upward = source + trans[level] * (upward - source)
            net[level] = net[level] - gsum(upward)
        return upward

    lax.fori_loop(0, strata // LEVEL_BLOCK, up, upward)
    heat[...] = jnp.zeros_like(heat)
    for h in range(2):
        change = net[h * levels : (h + 1) * levels] - net[h * levels + 1 : (h + 1) * levels + 1]
        heat[h, 0:levels] = jnp.sum(change, axis=1) / state[1, h * levels : (h + 1) * levels, :]
    copy = remote(heat.at[1 - side], other, ts_sem, tr_sem, {"sec": 1 - side})
    copy.start()
    copy.wait()
    own = heat[side] + other[...]
    fold = per // 2
    hi, lo = halves(jnp.concatenate([own, own], axis=0))
    spread = (mm(hi, member) + mm(lo, member)).T.reshape(n, 2, fold, LANES)
    back[...] = jnp.where(iota((n, fold, LANES), 2) // 64 == 0, spread[:, 0], spread[:, 1])
    copies = []
    for d in range(1, n):
        peer = lax.rem(me + d, n)
        copy = remote(back.at[peer], home.at[me], bo_sem.at[d], bi_sem.at[d], {"grp": peer})
        copy.start()
        copies.append(copy)
    home[me] = back[me]
    place = iota((n * fold, cols), 0)
    place = (place // fold) * (2 * fold) + lax.rem(place, fold) - pos[...]
    hots = [one_hot(place + q * fold == 0) for q in range(2)]
    for copy in copies:
        copy.wait()
    value = home[...].reshape(n * fold, LANES).T
    hi, lo = halves(value)
    total = None
    for q in range(2):
        here = slice(64 * q, 64 * (q + 1))
        part = mm(hi[here], hots[q]) + mm(lo[here], hots[q])
        total = part if total is None else total + part
    heating[...] = total[0:levels]


def one_kernel(n, *args):
    absorb = args[2]
    species, levels, cols = absorb.shape
    rows = -(-(levels + 3) // 8) * 8
    per = cols // n
    slab = 2 * per + per // 4
    wide = STEPS * HALO
    near = args[8].shape[0]
    gpoints, strata = args[10].shape[1:]
    span = cols + 2 * wide
    dma = pltpu.SemaphoreType.DMA
    f32 = jnp.float32
    return pl.pallas_call(
        functools.partial(device_kernel, n),
        out_shape=(
            jax.ShapeDtypeStruct((levels, cols), f32),
            jax.ShapeDtypeStruct(absorb.shape, f32),
        ),
        in_specs=[VMEM] * len(args),
        out_specs=(VMEM, VMEM),
        scratch_shapes=[
            pltpu.VMEM((3 * LANES, cols), f32),
            pltpu.VMEM((n, slab, LANES), f32),
            pltpu.VMEM((n, slab, LANES), f32),
            pltpu.VMEM((species, levels, wide), f32),
            pltpu.VMEM((species, levels, wide), f32),
            pltpu.VMEM((near, wide), jnp.int32),
            pltpu.VMEM((near, wide), jnp.int32),
            pltpu.VMEM((near, wide), f32),
            pltpu.VMEM((near, wide), f32),
            pltpu.VMEM((species * rows, span), f32),
            pltpu.VMEM((species * rows, span), f32),
            pltpu.VMEM((span // 256, 512, 256), jnp.bfloat16),
            pltpu.VMEM((span // 256, 512, 256), jnp.bfloat16),
            pltpu.VMEM((2, 3, cols // 4, LANES), f32),
            pltpu.VMEM((2 + species, -(-strata // 8) * 8, cols // 4), f32),
            pltpu.VMEM((strata // LEVEL_BLOCK, species * gpoints, LANES), f32),
            pltpu.VMEM((strata, gpoints, cols // 4), f32),
            pltpu.VMEM((strata + 1, 8, cols // 4), f32),
            pltpu.VMEM((2, 64, cols // 4), f32),
            pltpu.VMEM((64, cols // 4), f32),
            pltpu.VMEM((n, per // 2, LANES), f32),
            pltpu.VMEM((n, per // 2, LANES), f32),
            dma((n,)), dma((n,)), dma((6,)), dma((6,)), dma, dma, dma, dma, dma((n,)), dma((n,)),
        ],
        compiler_params=pltpu.CompilerParams(
            collective_id=0, has_side_effects=True, vmem_limit_bytes=48 << 20
        ),
        cost_estimate=pl.CostEstimate(flops=10**9, bytes_accessed=4 << 20, transcendentals=10**6),
    )(*args)


def folds_evenly(n, sides, levels, cols, species, gpoints):
    rows = -(-(levels + 3) // 8) * 8
    return (
        n > 3 and n % 4 == 0 and sides == 2 and species == 4
        and cols == n * 32 and cols == 4 * LANES and 2 * STEPS * HALO == cols
        and 6 * rows == 2 * LANES + 32 and gpoints % 8 == 0 and 2 * levels % LEVEL_BLOCK == 0
    )


def per_device(*args):
    (warmth, depth, absorb, ground, sun, mask, pos, memb, adj, blend, opacity, emission, sunshine) = args
    n = lax.axis_size("grp")
    levels, cols = warmth.shape
    gpoints = emission.shape[0]
    if not folds_evenly(n, lax.axis_size("sec"), levels, cols, absorb.shape[0], gpoints):
        return plain_device(*args)
    return one_kernel(
        n, warmth, depth, absorb, ground[None], sun[None], mask[None], pos, memb, adj, blend,
        opacity, emission[None], sunshine[None],
    )


def solution(mesh):
    in_specs = (
        P("sec", "grp"),
        P("sec", "grp"),
        P(None, "sec", "grp"),
        P("grp"),
        P("grp"),
        P("grp"),
        P("grp", None),
        P("grp", None),
        P(None, "grp"),
        P(None, "grp"),
        P(None, "sec", None),
        P("sec"),
        P("sec"),
    )
    out_specs = (P("sec", "grp"), P(None, "sec", "grp"))
    return jax.shard_map(
        per_device, mesh=mesh, in_specs=in_specs, out_specs=out_specs, check_vma=False
    )
```

```python
import functools

import jax
import jax.numpy as jnp
from jax import lax
from jax.experimental import pallas as pl
from jax.experimental.pallas import tpu as pltpu
from jax.sharding import PartitionSpec as P

STEPS = 4
LEVEL_BLOCK = 9
HALO = 64


DIFFUSE = 1.66
TOP = lax.Precision.HIGHEST


def padded(shard, sides, width):
    for axis, dim in sides:
        size, length = (lax.axis_size(axis), shard.shape[dim])
        up = [(i, (i + 1) % size) for i in range(size)]
        down = [(j, i) for i, j in up]
        last = lax.slice_in_dim(shard, length - width, length, axis=dim)
        first = lax.slice_in_dim(shard, 0, width, axis=dim)
        before = lax.ppermute(last, axis, up)
        after = lax.ppermute(first, axis, down)
        shard = jnp.concatenate([before, shard, after], axis=dim)
    return shard


def select_matrix(ids, count):
    return (ids[:, None] == jnp.arange(count, dtype=jnp.int32)[None, :]).astype(jnp.float32)


def pick_columns(values, selector):
    return lax.dot_general(values, selector, (((1,), (1,)), ((), ())), precision=TOP)


def optical(level_table, radiant_species, stratum_index):
    coeffs = lax.dynamic_index_in_dim(level_table, stratum_index, 0, keepdims=False)
    amounts = lax.dynamic_index_in_dim(radiant_species, stratum_index, 1, keepdims=False)
    optical_depth = coeffs[0][:, None] * amounts[0][None, :]
    for species in range(1, coeffs.shape[0]):
        optical_depth = optical_depth + coeffs[species][:, None] * amounts[species][None, :]
    return optical_depth


def compute_flux_heating(
    radiant_warmth,
    radiant_depth,
    radiant_species,
    radiant_ground,
    sunlight_incline,
    incoming_sunshine,
    opacity_table,
    emission_share,
    sunshine_share,
):
    strata_range, radiant_span = radiant_warmth.shape
    blocks = strata_range // LEVEL_BLOCK
    gpoints = emission_share.shape[0]
    block_ids = jnp.arange(blocks, dtype=jnp.int32)
    level_table = jnp.transpose(opacity_table, (2, 0, 1))

    def layer_terms(stratum_index):
        optical_depth = optical(level_table, radiant_species, stratum_index)
        stratum_warmth = lax.dynamic_index_in_dim(radiant_warmth, stratum_index, 0, keepdims=False)
        source = emission_share[:, None] * (stratum_warmth**4)[None, :]
        return (optical_depth, jnp.exp(-DIFFUSE * optical_depth), source)

    def down_block(fluxes, block_id):
        thermal, direct = fluxes
        thermal_rows = []
        direct_rows = []
        for inner_id in range(LEVEL_BLOCK):
            optical_depth, transmit, source = layer_terms(block_id * LEVEL_BLOCK + inner_id)
            thermal = transmit * thermal + (1.0 - transmit) * source
            direct = direct * jnp.exp(-optical_depth / sunlight_incline[None, :])
            thermal_rows.append(jnp.sum(thermal, axis=0))
            direct_rows.append(jnp.sum(direct, axis=0))
        return ((thermal, direct), (jnp.stack(thermal_rows), jnp.stack(direct_rows)))

    down_init = (
        jnp.zeros((gpoints, radiant_span), jnp.float32),
        sunshine_share[:, None] * incoming_sunshine[None, :],
    )
    final_down, (down_rows, direct_rows) = lax.scan(down_block, down_init, block_ids)
    thermal_down = jnp.concatenate(
        [jnp.zeros((1, radiant_span), jnp.float32), down_rows.reshape(strata_range, radiant_span)],
        axis=0,
    )
    direct_down = jnp.concatenate(
        [jnp.sum(down_init[1], axis=0)[None], direct_rows.reshape(strata_range, radiant_span)],
        axis=0,
    )

    def up_block(upward, block_id):
        upward_rows = []
        for inner_id in range(LEVEL_BLOCK - 1, -1, -1):
            optical_depth, transmit, source = layer_terms(block_id * LEVEL_BLOCK + inner_id)
            upward = transmit * upward + (1.0 - transmit) * source
            upward_rows.append(jnp.sum(upward, axis=0))
        return (upward, jnp.stack(upward_rows[::-1]))

    up_init = emission_share[:, None] * (radiant_ground**4)[None, :]
    final_up, up_rows = lax.scan(up_block, up_init, block_ids, reverse=True)
    upward_flux = jnp.concatenate(
        [up_rows.reshape(strata_range, radiant_span), jnp.sum(up_init, axis=0)[None]], axis=0
    )
    net_flux = thermal_down - upward_flux + direct_down
    return (net_flux[:-1] - net_flux[1:]) / radiant_depth


def plain_device(
    stratum_warmth_anomaly,
    pressure_depth,
    absorber_amounts,
    ground_warmth_anomaly,
    sun_elevation_factor,
    daytime_mask,
    dispatch_position,
    arrival_membership,
    adjacency_table,
    blending_coefficient,
    opacity_table,
    emission_share,
    sunshine_share,
):
    cell_sequence = stratum_warmth_anomaly.shape[1]
    position = dispatch_position[0]
    placing = select_matrix(position, cell_sequence)
    state_bundle = jnp.concatenate(
        [stratum_warmth_anomaly[None], pressure_depth[None], absorber_amounts], axis=0
    )
    surface = jnp.stack(
        [
            ground_warmth_anomaly,
            sun_elevation_factor,
            daytime_mask.astype(jnp.float32) * sun_elevation_factor,
        ],
        axis=0,
    )[:, None, :]
    packed = jnp.dot(state_bundle.reshape(-1, cell_sequence), placing, precision=TOP).reshape(
        state_bundle.shape
    )
    packed_surface = jnp.dot(surface.reshape(3, cell_sequence), placing, precision=TOP).reshape(
        surface.shape
    )
    groups_dev = cell_sequence // 4
    group_ids = arrival_membership[0] // 4
    half_arrived, arrived_surface = (
        lax.all_to_all(packed, "grp", split_axis=2, concat_axis=2, tiled=True),
        lax.all_to_all(packed_surface, "grp", split_axis=2, concat_axis=2, tiled=True),
    )
    arrived = lax.all_gather(half_arrived, "sec", axis=1, tiled=True)
    selector = select_matrix(group_ids, groups_dev)
    member = selector * 0.25
    flattened = arrived.reshape(-1, cell_sequence)
    pooled = jnp.dot(flattened, member, precision=TOP).reshape(
        arrived.shape[0], arrived.shape[1], groups_dev
    )
    pooled_surface = jnp.dot(arrived_surface.reshape(3, cell_sequence), member, precision=TOP)
    heat_part = compute_flux_heating(
        pooled[0],
        pooled[1],
        pooled[2:],
        pooled_surface[0],
        pooled_surface[1],
        pooled_surface[2],
        opacity_table,
        emission_share,
        sunshine_share,
    )
    slot_heat = pick_columns(heat_part, selector)
    returned = lax.all_to_all(slot_heat, "grp", split_axis=1, concat_axis=1, tiled=True)
    own_heat = pick_columns(returned, placing)
    heating = lax.psum_scatter(own_heat, "sec", scatter_dimension=0, tiled=True)
    extended_span = cell_sequence + 2 * HALO
    source_rows = jnp.arange(extended_span, dtype=jnp.int32)[:, None]
    blend_matrix = jnp.zeros((extended_span, cell_sequence), jnp.float32)
    for near_id in range(adjacency_table.shape[0]):
        blend_matrix = blend_matrix + jnp.where(
            adjacency_table[near_id][None, :] == source_rows,
            blending_coefficient[near_id][None, :],
            0.0,
        )
    centre_rows = jnp.arange(cell_sequence, dtype=jnp.int32)[None, :] + HALO
    weight_total = jnp.sum(blending_coefficient, axis=0)
    blend_matrix = blend_matrix - jnp.where(source_rows == centre_rows, weight_total[None, :], 0.0)
    mixed = absorber_amounts
    for step_id in range(STEPS):
        extended = padded(mixed, (("grp", 2),), HALO)
        update = jnp.dot(extended.reshape(-1, extended_span), blend_matrix, precision=TOP).reshape(
            mixed.shape
        )
        mixed = mixed + update
    return (heating, mixed)


LANES = 128
NT = (((1,), (1,)), ((), ()))
VMEM = pl.BlockSpec(memory_space=pltpu.VMEM)
MESH = pl.DeviceIdType.MESH


def halves(value):
    high = value.astype(jnp.bfloat16)
    low = (value - high.astype(jnp.float32)).astype(jnp.bfloat16)
    return high, low


def iota(shape, dim):
    return lax.broadcasted_iota(jnp.int32, shape, dim)


def one_hot(cond):
    return jnp.where(cond, 1.0, 0.0).astype(jnp.bfloat16)


def mm(left, right, dims=(((1,), (0,)), ((), ()))):
    return lax.dot_general(left, right, dims, preferred_element_type=jnp.float32)


def flipped(me, distance):
    peer, bit = me, 1
    while bit <= distance:
        if distance & bit:
            peer = peer + bit - 2 * bit * lax.rem(me // bit, 2)
        bit *= 2
    return peer


def greet(n):
    me, side = lax.axis_index("grp"), lax.axis_index("sec")
    barrier = pltpu.get_barrier_semaphore()
    for d in range(n - 1, 0, -1):
        pl.semaphore_signal(barrier, inc=1, device_id={"grp": flipped(me, d)}, device_id_type=MESH)
    pl.semaphore_signal(barrier, inc=1, device_id={"sec": 1 - side}, device_id_type=MESH)
    return me, side, barrier


def remote(src, dst, send_sem, recv_sem, device):
    return pltpu.make_async_remote_copy(
        src_ref=src, dst_ref=dst, send_sem=send_sem, recv_sem=recv_sem,
        device_id=device, device_id_type=MESH,
    )


def device_kernel(
    n, temp, depth, absorb, ground, sun, mask, pos, memb, adj, blend,
    opacity, emission, sunshine, heating, mixed_out,
    data, send, recv, halo_l, halo_r, adj_l, adj_r, blend_l, blend_r,
    grid_a, grid_b, mix_hi, mix_lo, pooled,
    state, opac, trans, net, heat, other, back, home,
    out_sem, in_sem, hs_sem, hr_sem, ps_sem, pr_sem, ts_sem, tr_sem, bo_sem, bi_sem,
):
    species, levels, cols = absorb.shape
    rows = -(-(levels + 3) // 8) * 8
    per = cols // n
    pack = per // 4
    rads = cols // 4
    wide = STEPS * HALO
    me, side, barrier = greet(n)
    right, left = lax.rem(me + 1, n), lax.rem(me + n - 1, n)

    halo = []
    for k, (src, to_left, to_right) in enumerate(
        ((absorb, halo_r, halo_l), (adj, adj_r, adj_l), (blend, blend_r, blend_l))
    ):
        lead = (slice(None),) * (len(src.shape) - 1)
        first, last = src.at[lead + (pl.ds(0, wide),)], src.at[lead + (pl.ds(cols - wide, wide),)]
        halo.append(remote(first, to_left, hs_sem.at[2 * k], hr_sem.at[2 * k], {"grp": left}))
        halo.append(remote(last, to_right, hs_sem.at[2 * k + 1], hr_sem.at[2 * k + 1], {"grp": right}))

    data[...] = jnp.zeros_like(data)
    data[0:levels, :] = temp[...]
    data[rows : rows + levels, :] = depth[...]
    for s in range(species):
        data[(2 + s) * rows : (2 + s) * rows + levels, :] = absorb[s]
    data[levels : levels + 1, :] = ground[...]
    data[levels + 1 : levels + 2, :] = sun[...]
    data[levels + 2 : levels + 3, :] = mask[...].astype(jnp.float32) * sun[...]
    rest = data[2 * LANES : 2 * LANES + 32, :]
    for q in range(1, 4):
        data[2 * LANES + 32 * q : 2 * LANES + 32 * (q + 1), :] = rest
    data_hi, data_lo = halves(data[...])
    lane_block = iota((4, pack, LANES), 2) // 32
    slot_row = iota((per, cols), 0) - pos[...]
    order = [*range(n // 8, n // 4), *range(n // 8 - 1, -1, -1)]
    copies = []
    for turn, c in enumerate(order):
        peers = [flipped(me, d) for d in range(4 * c, 4 * c + 4)]
        hot = jnp.concatenate([one_hot(slot_row + peer * per == 0) for peer in peers], axis=0)
        out = mm(hot, data_hi, NT) + mm(hot, data_lo, NT)
        send[4 * c : 4 * c + 4, 0:per, :] = out[:, 0:LANES].reshape(4, per, LANES)
        send[4 * c : 4 * c + 4, per : 2 * per, :] = out[:, LANES : 2 * LANES].reshape(4, per, LANES)
        tail = out[:, 2 * LANES :].reshape(4, 4, pack, LANES)
        folded = jnp.where(lane_block == 0, tail[:, 0], 0.0)
        for q in range(1, 4):
            folded = jnp.where(lane_block == q, tail[:, q], folded)
        send[4 * c : 4 * c + 4, 2 * per :, :] = folded
        if turn == 0:
            pl.semaphore_wait(barrier, n)
        for d in range(max(4 * c, 1), 4 * c + 4):
            copy = remote(
                send.at[d], recv.at[me], out_sem.at[d], in_sem.at[d], {"grp": peers[d - 4 * c]}
            )
            copy.start()
            copies.append(copy)
        if turn == 0:
            for copy in halo:
                copy.start()
    recv[me] = send[0]

    grid_a[...] = jnp.zeros_like(grid_a)
    grid_b[...] = jnp.zeros_like(grid_b)
    for s in range(species):
        grid_a[s * rows : s * rows + levels, wide : wide + cols] = absorb[s]
    for copy in halo:
        copy.wait()
    for s in range(species):
        grid_a[s * rows : s * rows + levels, 0:wide] = halo_l[s]
        grid_a[s * rows : s * rows + levels, wide + cols :] = halo_r[s]
    span = cols + 2 * wide
    tables = (
        (adj_l[...] - HALO + wide - cols, blend_l[...]),
        (adj[...] - HALO + wide, blend[...]),
        (adj_r[...] - HALO + wide + cols, blend_r[...]),
    )
    table = jnp.concatenate([t[0] for t in tables], axis=1)
    weight = jnp.concatenate([t[1] for t in tables], axis=1)
    total = jnp.sum(weight, axis=0, keepdims=True)
    width = 256
    windows = []
    for b in range(span // width):
        low, high = max(0, width * b - LANES), min(span, width * (b + 1) + LANES)
        windows.append((low, high))
        source = iota((high - low, width), 0) + low
        matrix = jnp.zeros((high - low, width), jnp.float32)
        here = slice(width * b, width * (b + 1))
        for k in range(table.shape[0]):
            matrix = matrix + jnp.where(table[k : k + 1, here] == source, weight[k : k + 1, here], 0.0)
        hi, lo = halves(matrix)
        mix_hi[b, 0 : high - low, :] = hi
        mix_lo[b, 0 : high - low, :] = lo
    old, new = grid_a, grid_b
    for step in range(STEPS):
        blocks = range(span // width)
        if step == STEPS - 1:
            blocks = range(wide // width, (wide + cols) // width)
        for b in blocks:
            low, high = windows[b]
            here = slice(width * b, width * (b + 1))
            hi, lo = halves(old[:, low:high])
            left_hi = mix_hi[b, 0 : high - low, :]
            update = mm(hi, left_hi) + mm(lo, left_hi) + mm(hi, mix_lo[b, 0 : high - low, :])
            centre = old[:, here]
            new[:, here] = centre + (update - total[:, here] * centre)
        old, new = new, old
    for s in range(species):
        mixed_out[s] = old[s * rows : s * rows + levels, wide : wide + cols]

    gpoints = emission.shape[1]
    strata = opacity.shape[2]
    for b in range(strata // LEVEL_BLOCK):
        for k in range(species):
            opac[b, k * gpoints : (k + 1) * gpoints, 0:LEVEL_BLOCK] = opacity[
                k, :, b * LEVEL_BLOCK : (b + 1) * LEVEL_BLOCK
            ]
    diagonal = iota((gpoints, gpoints), 0) == iota((gpoints, gpoints), 1)
    share = jnp.sum(jnp.where(diagonal, emission[...], 0.0), axis=1, keepdims=True)
    sunny = jnp.sum(jnp.where(diagonal, sunshine[...], 0.0), axis=1, keepdims=True)
    share = jnp.broadcast_to(share, (gpoints, rads))
    member = one_hot(iota((rads, cols), 0) == lax.shift_right_logical(memb[...], 2))

    for copy in copies:
        copy.wait()
    whole = recv[...]
    parts = [whole[:, 0:per, :].reshape(cols, LANES), whole[:, per : 2 * per, :].reshape(cols, LANES)]
    tail = whole[:, 2 * per :, :]
    big_block = iota((n, pack, LANES), 2) // 32
    tail = jnp.stack([jnp.where(big_block == q, tail, 0.0) for q in range(4)], axis=1)
    parts.append(tail.reshape(cols, LANES))
    across = []
    for k, part in enumerate(parts):
        hi, lo = halves(part)
        pooled[side, k] = (mm(member, hi) + mm(member, lo)) * 0.25
        copy = remote(
            pooled.at[side, k], pooled.at[side, k], ps_sem.at[k], pr_sem.at[k], {"sec": 1 - side}
        )
        copy.start()
        across.append(copy)

    def unfold(h):
        tail = pooled[h, 2].T
        tail = tail[0:32] + tail[32:64] + tail[64:96] + tail[96:128]
        field = jnp.concatenate([pooled[h, 0].T, pooled[h, 1].T, tail], axis=0)
        for k in range(2 + species):
            state[k, h, 0:levels, :] = field[k * rows : k * rows + levels]
        return field[levels : levels + 3]

    surface = unfold(side)
    for copy in across:
        copy.wait()
    unfold(1 - side)

    def fourth(value):
        square = value * value
        return square * square

    def gsum(value):
        return jnp.sum(value.reshape(gpoints // 8, 8, rads), axis=0)

    slant = -1.0 / surface[1:2]
    state[0, :, 0:levels, :] = fourth(state[0, :, 0:levels, :])

    def down(b, fluxes):
        thermal, direct = fluxes
        coeffs = opac[b]
        for i in range(LEVEL_BLOCK):
            level = b * LEVEL_BLOCK + i
            half = level // levels
            tau = None
            for k in range(species):
                part = coeffs[k * gpoints : (k + 1) * gpoints, i : i + 1] * state[2 + k, half, pl.ds(level - half * levels, 1), :]
                tau = part if tau is None else tau + part
            transmit = jnp.exp(-DIFFUSE * tau)
            trans[level] = transmit
            source = share * state[0, half, pl.ds(level - half * levels, 1), :]
            thermal = source + transmit * (thermal - source)
            direct = direct * jnp.exp(tau * slant)
            net[level + 1] = gsum(thermal + direct)
        return thermal, direct

    direct = sunny * surface[2:3]
    net[0] = gsum(direct)
    lax.fori_loop(0, strata // LEVEL_BLOCK, down, (jnp.zeros((gpoints, rads), jnp.float32), direct))
    upward = share * fourth(surface[0:1])
    net[strata] = net[strata] - gsum(upward)

    def up(b, upward):
        for i in range(LEVEL_BLOCK):
            level = strata - 1 - (b * LEVEL_BLOCK + i)
            half = level // levels
            source = share * state[0, half, pl.ds(level - half * levels, 1), :]
            upward = source + trans[level] * (upward - source)
            net[level] = net[level] - gsum(upward)
        return upward

    lax.fori_loop(0, strata // LEVEL_BLOCK, up, upward)
    heat[...] = jnp.zeros_like(heat)
    for h in range(2):
        change = net[h * levels : (h + 1) * levels] - net[h * levels + 1 : (h + 1) * levels + 1]
        heat[h, 0:levels] = jnp.sum(change, axis=1) / state[1, h, 0:levels, :]
    copy = remote(heat.at[1 - side], other, ts_sem, tr_sem, {"sec": 1 - side})
    copy.start()
    copy.wait()
    own = heat[side] + other[...]
    fold = per // 2
    hi, lo = halves(jnp.concatenate([own, own], axis=0))
    spread = (mm(hi, member) + mm(lo, member)).T.reshape(n, 2, fold, LANES)
    back[...] = jnp.where(iota((n, fold, LANES), 2) // 64 == 0, spread[:, 0], spread[:, 1])
    copies = []
    for d in [*range(n // 2, n), *range(n // 2 - 1, 0, -1)]:
        peer = flipped(me, d)
        copy = remote(back.at[peer], home.at[me], bo_sem.at[d], bi_sem.at[d], {"grp": peer})
        copy.start()
        copies.append(copy)
    home[me] = back[me]
    place = iota((n * fold, cols), 0)
    place = (place // fold) * (2 * fold) + lax.rem(place, fold) - pos[...]
    hots = [one_hot(place + q * fold == 0) for q in range(2)]
    for copy in copies:
        copy.wait()
    value = home[...].reshape(n * fold, LANES).T
    hi, lo = halves(value)
    total = None
    for q in range(2):
        here = slice(64 * q, 64 * (q + 1))
        part = mm(hi[here], hots[q]) + mm(lo[here], hots[q])
        total = part if total is None else total + part
    heating[...] = total[0:levels]


def one_kernel(n, *args):
    absorb = args[2]
    species, levels, cols = absorb.shape
    rows = -(-(levels + 3) // 8) * 8
    per = cols // n
    slab = 2 * per + per // 4
    wide = STEPS * HALO
    near = args[8].shape[0]
    gpoints, strata = args[10].shape[1:]
    span = cols + 2 * wide
    dma = pltpu.SemaphoreType.DMA
    f32 = jnp.float32
    return pl.pallas_call(
        functools.partial(device_kernel, n),
        out_shape=(
            jax.ShapeDtypeStruct((levels, cols), f32),
            jax.ShapeDtypeStruct(absorb.shape, f32),
        ),
        in_specs=[VMEM] * len(args),
        out_specs=(VMEM, VMEM),
        scratch_shapes=[
            pltpu.VMEM((3 * LANES, cols), f32),
            pltpu.VMEM((n, slab, LANES), f32),
            pltpu.VMEM((n, slab, LANES), f32),
            pltpu.VMEM((species, levels, wide), f32),
            pltpu.VMEM((species, levels, wide), f32),
            pltpu.VMEM((near, wide), jnp.int32),
            pltpu.VMEM((near, wide), jnp.int32),
            pltpu.VMEM((near, wide), f32),
            pltpu.VMEM((near, wide), f32),
            pltpu.VMEM((species * rows, span), f32),
            pltpu.VMEM((species * rows, span), f32),
            pltpu.VMEM((span // 256, 512, 256), jnp.bfloat16),
            pltpu.VMEM((span // 256, 512, 256), jnp.bfloat16),
            pltpu.VMEM((2, 3, cols // 4, LANES), f32),
            pltpu.VMEM((2 + species, 2, rows, cols // 4), f32),
            pltpu.VMEM((strata // LEVEL_BLOCK, species * gpoints, LANES), f32),
            pltpu.VMEM((strata, gpoints, cols // 4), f32),
            pltpu.VMEM((strata + 1, 8, cols // 4), f32),
            pltpu.VMEM((2, 64, cols // 4), f32),
            pltpu.VMEM((64, cols // 4), f32),
            pltpu.VMEM((n, per // 2, LANES), f32),
            pltpu.VMEM((n, per // 2, LANES), f32),
            dma((n,)), dma((n,)), dma((6,)), dma((6,)), dma((3,)), dma((3,)), dma, dma, dma((n,)), dma((n,)),
        ],
        compiler_params=pltpu.CompilerParams(
            collective_id=0, has_side_effects=True, vmem_limit_bytes=48 << 20
        ),
        cost_estimate=pl.CostEstimate(flops=10**9, bytes_accessed=4 << 20, transcendentals=10**6),
    )(*args)


def folds_evenly(n, sides, levels, cols, species, gpoints):
    rows = -(-(levels + 3) // 8) * 8
    return (
        n > 7 and n & (n - 1) == 0 and sides == 2 and species == 4
        and cols == n * 32 and cols == 4 * LANES and 2 * STEPS * HALO == cols
        and 6 * rows == 2 * LANES + 32 and gpoints % 8 == 0 and 2 * levels % LEVEL_BLOCK == 0
    )


def per_device(*args):
    (warmth, depth, absorb, ground, sun, mask, pos, memb, adj, blend, opacity, emission, sunshine) = args
    n = lax.axis_size("grp")
    levels, cols = warmth.shape
    gpoints = emission.shape[0]
    if not folds_evenly(n, lax.axis_size("sec"), levels, cols, absorb.shape[0], gpoints):
        return plain_device(*args)
    return one_kernel(
        n, warmth, depth, absorb, ground[None], sun[None], mask[None], pos, memb, adj, blend,
        opacity, emission[None], sunshine[None],
    )


def solution(mesh):
    in_specs = (
        P("sec", "grp"),
        P("sec", "grp"),
        P(None, "sec", "grp"),
        P("grp"),
        P("grp"),
        P("grp"),
        P("grp", None),
        P("grp", None),
        P(None, "grp"),
        P(None, "grp"),
        P(None, "sec", None),
        P("sec"),
        P("sec"),
    )
    out_specs = (P("sec", "grp"), P(None, "sec", "grp"))
    return jax.shard_map(
        per_device, mesh=mesh, in_specs=in_specs, out_specs=out_specs, check_vma=False
    )
```

```python
import functools

import jax
import jax.numpy as jnp
from jax import lax
from jax.experimental import pallas as pl
from jax.experimental.pallas import tpu as pltpu
from jax.sharding import PartitionSpec as P

STEPS = 4
LEVEL_BLOCK = 9
HALO = 64


DIFFUSE = 1.66
TOP = lax.Precision.HIGHEST


def padded(shard, sides, width):
    for axis, dim in sides:
        size, length = (lax.axis_size(axis), shard.shape[dim])
        up = [(i, (i + 1) % size) for i in range(size)]
        down = [(j, i) for i, j in up]
        last = lax.slice_in_dim(shard, length - width, length, axis=dim)
        first = lax.slice_in_dim(shard, 0, width, axis=dim)
        before = lax.ppermute(last, axis, up)
        after = lax.ppermute(first, axis, down)
        shard = jnp.concatenate([before, shard, after], axis=dim)
    return shard


def select_matrix(ids, count):
    return (ids[:, None] == jnp.arange(count, dtype=jnp.int32)[None, :]).astype(jnp.float32)


def pick_columns(values, selector):
    return lax.dot_general(values, selector, (((1,), (1,)), ((), ())), precision=TOP)


def optical(level_table, radiant_species, stratum_index):
    coeffs = lax.dynamic_index_in_dim(level_table, stratum_index, 0, keepdims=False)
    amounts = lax.dynamic_index_in_dim(radiant_species, stratum_index, 1, keepdims=False)
    optical_depth = coeffs[0][:, None] * amounts[0][None, :]
    for species in range(1, coeffs.shape[0]):
        optical_depth = optical_depth + coeffs[species][:, None] * amounts[species][None, :]
    return optical_depth


def compute_flux_heating(
    radiant_warmth,
    radiant_depth,
    radiant_species,
    radiant_ground,
    sunlight_incline,
    incoming_sunshine,
    opacity_table,
    emission_share,
    sunshine_share,
):
    strata_range, radiant_span = radiant_warmth.shape
    blocks = strata_range // LEVEL_BLOCK
    gpoints = emission_share.shape[0]
    block_ids = jnp.arange(blocks, dtype=jnp.int32)
    level_table = jnp.transpose(opacity_table, (2, 0, 1))

    def layer_terms(stratum_index):
        optical_depth = optical(level_table, radiant_species, stratum_index)
        stratum_warmth = lax.dynamic_index_in_dim(radiant_warmth, stratum_index, 0, keepdims=False)
        source = emission_share[:, None] * (stratum_warmth**4)[None, :]
        return (optical_depth, jnp.exp(-DIFFUSE * optical_depth), source)

    def down_block(fluxes, block_id):
        thermal, direct = fluxes
        thermal_rows = []
        direct_rows = []
        for inner_id in range(LEVEL_BLOCK):
            optical_depth, transmit, source = layer_terms(block_id * LEVEL_BLOCK + inner_id)
            thermal = transmit * thermal + (1.0 - transmit) * source
            direct = direct * jnp.exp(-optical_depth / sunlight_incline[None, :])
            thermal_rows.append(jnp.sum(thermal, axis=0))
            direct_rows.append(jnp.sum(direct, axis=0))
        return ((thermal, direct), (jnp.stack(thermal_rows), jnp.stack(direct_rows)))

    down_init = (
        jnp.zeros((gpoints, radiant_span), jnp.float32),
        sunshine_share[:, None] * incoming_sunshine[None, :],
    )
    final_down, (down_rows, direct_rows) = lax.scan(down_block, down_init, block_ids)
    thermal_down = jnp.concatenate(
        [jnp.zeros((1, radiant_span), jnp.float32), down_rows.reshape(strata_range, radiant_span)],
        axis=0,
    )
    direct_down = jnp.concatenate(
        [jnp.sum(down_init[1], axis=0)[None], direct_rows.reshape(strata_range, radiant_span)],
        axis=0,
    )

    def up_block(upward, block_id):
        upward_rows = []
        for inner_id in range(LEVEL_BLOCK - 1, -1, -1):
            optical_depth, transmit, source = layer_terms(block_id * LEVEL_BLOCK + inner_id)
            upward = transmit * upward + (1.0 - transmit) * source
            upward_rows.append(jnp.sum(upward, axis=0))
        return (upward, jnp.stack(upward_rows[::-1]))

    up_init = emission_share[:, None] * (radiant_ground**4)[None, :]
    final_up, up_rows = lax.scan(up_block, up_init, block_ids, reverse=True)
    upward_flux = jnp.concatenate(
        [up_rows.reshape(strata_range, radiant_span), jnp.sum(up_init, axis=0)[None]], axis=0
    )
    net_flux = thermal_down - upward_flux + direct_down
    return (net_flux[:-1] - net_flux[1:]) / radiant_depth


def plain_device(
    stratum_warmth_anomaly,
    pressure_depth,
    absorber_amounts,
    ground_warmth_anomaly,
    sun_elevation_factor,
    daytime_mask,
    dispatch_position,
    arrival_membership,
    adjacency_table,
    blending_coefficient,
    opacity_table,
    emission_share,
    sunshine_share,
):
    cell_sequence = stratum_warmth_anomaly.shape[1]
    position = dispatch_position[0]
    placing = select_matrix(position, cell_sequence)
    state_bundle = jnp.concatenate(
        [stratum_warmth_anomaly[None], pressure_depth[None], absorber_amounts], axis=0
    )
    surface = jnp.stack(
        [
            ground_warmth_anomaly,
            sun_elevation_factor,
            daytime_mask.astype(jnp.float32) * sun_elevation_factor,
        ],
        axis=0,
    )[:, None, :]
    packed = jnp.dot(state_bundle.reshape(-1, cell_sequence), placing, precision=TOP).reshape(
        state_bundle.shape
    )
    packed_surface = jnp.dot(surface.reshape(3, cell_sequence), placing, precision=TOP).reshape(
        surface.shape
    )
    groups_dev = cell_sequence // 4
    group_ids = arrival_membership[0] // 4
    half_arrived, arrived_surface = (
        lax.all_to_all(packed, "grp", split_axis=2, concat_axis=2, tiled=True),
        lax.all_to_all(packed_surface, "grp", split_axis=2, concat_axis=2, tiled=True),
    )
    arrived = lax.all_gather(half_arrived, "sec", axis=1, tiled=True)
    selector = select_matrix(group_ids, groups_dev)
    member = selector * 0.25
    flattened = arrived.reshape(-1, cell_sequence)
    pooled = jnp.dot(flattened, member, precision=TOP).reshape(
        arrived.shape[0], arrived.shape[1], groups_dev
    )
    pooled_surface = jnp.dot(arrived_surface.reshape(3, cell_sequence), member, precision=TOP)
    heat_part = compute_flux_heating(
        pooled[0],
        pooled[1],
        pooled[2:],
        pooled_surface[0],
        pooled_surface[1],
        pooled_surface[2],
        opacity_table,
        emission_share,
        sunshine_share,
    )
    slot_heat = pick_columns(heat_part, selector)
    returned = lax.all_to_all(slot_heat, "grp", split_axis=1, concat_axis=1, tiled=True)
    own_heat = pick_columns(returned, placing)
    heating = lax.psum_scatter(own_heat, "sec", scatter_dimension=0, tiled=True)
    extended_span = cell_sequence + 2 * HALO
    source_rows = jnp.arange(extended_span, dtype=jnp.int32)[:, None]
    blend_matrix = jnp.zeros((extended_span, cell_sequence), jnp.float32)
    for near_id in range(adjacency_table.shape[0]):
        blend_matrix = blend_matrix + jnp.where(
            adjacency_table[near_id][None, :] == source_rows,
            blending_coefficient[near_id][None, :],
            0.0,
        )
    centre_rows = jnp.arange(cell_sequence, dtype=jnp.int32)[None, :] + HALO
    weight_total = jnp.sum(blending_coefficient, axis=0)
    blend_matrix = blend_matrix - jnp.where(source_rows == centre_rows, weight_total[None, :], 0.0)
    mixed = absorber_amounts
    for step_id in range(STEPS):
        extended = padded(mixed, (("grp", 2),), HALO)
        update = jnp.dot(extended.reshape(-1, extended_span), blend_matrix, precision=TOP).reshape(
            mixed.shape
        )
        mixed = mixed + update
    return (heating, mixed)


LANES = 128
NT = (((1,), (1,)), ((), ()))
VMEM = pl.BlockSpec(memory_space=pltpu.VMEM)
MESH = pl.DeviceIdType.MESH


def halves(value):
    high = value.astype(jnp.bfloat16)
    low = (value - high.astype(jnp.float32)).astype(jnp.bfloat16)
    return high, low


def iota(shape, dim):
    return lax.broadcasted_iota(jnp.int32, shape, dim)


def one_hot(cond):
    return jnp.where(cond, 1.0, 0.0).astype(jnp.bfloat16)


def mm(left, right, dims=(((1,), (0,)), ((), ()))):
    return lax.dot_general(left, right, dims, preferred_element_type=jnp.float32)


def flipped(me, distance):
    peer, bit = me, 1
    while bit <= distance:
        if distance & bit:
            peer = peer + bit - 2 * bit * lax.rem(me // bit, 2)
        bit *= 2
    return peer


def greet(n):
    me, side = lax.axis_index("grp"), lax.axis_index("sec")
    barrier = pltpu.get_barrier_semaphore()
    for d in range(n - 1, 0, -1):
        pl.semaphore_signal(barrier, inc=1, device_id={"grp": flipped(me, d)}, device_id_type=MESH)
    pl.semaphore_signal(barrier, inc=1, device_id={"sec": 1 - side}, device_id_type=MESH)
    return me, side, barrier


def remote(src, dst, send_sem, recv_sem, device):
    return pltpu.make_async_remote_copy(
        src_ref=src, dst_ref=dst, send_sem=send_sem, recv_sem=recv_sem,
        device_id=device, device_id_type=MESH,
    )


def device_kernel(
    n, temp, depth, absorb, ground, sun, mask, pos, memb, adj, blend,
    opacity, emission, sunshine, heating, mixed_out,
    data, send, recv, halo_l, halo_r, adj_l, adj_r, blend_l, blend_r,
    grid_a, grid_b, mix_hi, mix_lo, pooled,
    state, opac, trans, net, heat, other, back, home, pair,
    out_sem, in_sem, hs_sem, hr_sem, ps_sem, pr_sem, ts_sem, tr_sem, bo_sem, bi_sem,
):
    species, levels, cols = absorb.shape
    rows = -(-(levels + 3) // 8) * 8
    per = cols // n
    pack = per // 4
    rads = cols // 4
    wide = STEPS * HALO
    me, side, barrier = greet(n)
    right, left = lax.rem(me + 1, n), lax.rem(me + n - 1, n)

    halo = []
    for k, (src, to_left, to_right) in enumerate(
        ((absorb, halo_r, halo_l), (adj, adj_r, adj_l), (blend, blend_r, blend_l))
    ):
        lead = (slice(None),) * (len(src.shape) - 1)
        first, last = src.at[lead + (pl.ds(0, wide),)], src.at[lead + (pl.ds(cols - wide, wide),)]
        halo.append(remote(first, to_left, hs_sem.at[2 * k], hr_sem.at[2 * k], {"grp": left}))
        halo.append(remote(last, to_right, hs_sem.at[2 * k + 1], hr_sem.at[2 * k + 1], {"grp": right}))

    data[...] = jnp.zeros_like(data)
    data[0:levels, :] = temp[...]
    data[rows : rows + levels, :] = depth[...]
    for s in range(species):
        data[(2 + s) * rows : (2 + s) * rows + levels, :] = absorb[s]
    data[levels : levels + 1, :] = ground[...]
    data[levels + 1 : levels + 2, :] = sun[...]
    data[levels + 2 : levels + 3, :] = mask[...].astype(jnp.float32) * sun[...]
    rest = data[2 * LANES : 2 * LANES + 32, :]
    for q in range(1, 4):
        data[2 * LANES + 32 * q : 2 * LANES + 32 * (q + 1), :] = rest
    data_hi, data_lo = halves(data[...])
    lane_block = iota((4, pack, LANES), 2) // 32
    slot_row = iota((per, cols), 0) - pos[...]
    order = [*range(n // 8, n // 4), *range(n // 8 - 1, -1, -1)]
    copies = []
    for turn, c in enumerate(order):
        peers = [flipped(me, d) for d in range(4 * c, 4 * c + 4)]
        hot = jnp.concatenate([one_hot(slot_row + peer * per == 0) for peer in peers], axis=0)
        out = mm(hot, data_hi, NT) + mm(hot, data_lo, NT)
        send[4 * c : 4 * c + 4, 0:per, :] = out[:, 0:LANES].reshape(4, per, LANES)
        send[4 * c : 4 * c + 4, per : 2 * per, :] = out[:, LANES : 2 * LANES].reshape(4, per, LANES)
        tail = out[:, 2 * LANES :].reshape(4, 4, pack, LANES)
        folded = jnp.where(lane_block == 0, tail[:, 0], 0.0)
        for q in range(1, 4):
            folded = jnp.where(lane_block == q, tail[:, q], folded)
        send[4 * c : 4 * c + 4, 2 * per :, :] = folded
        if turn == 0:
            pl.semaphore_wait(barrier, n)
        for d in range(max(4 * c, 1), 4 * c + 4):
            copy = remote(
                send.at[d], recv.at[me], out_sem.at[d], in_sem.at[d], {"grp": peers[d - 4 * c]}
            )
            copy.start()
            copies.append(copy)
        if turn == 0:
            for copy in halo:
                copy.start()
    recv[me] = send[0]

    grid_a[...] = jnp.zeros_like(grid_a)
    grid_b[...] = jnp.zeros_like(grid_b)
    for s in range(species):
        grid_a[s * rows : s * rows + levels, wide : wide + cols] = absorb[s]
    for copy in halo:
        copy.wait()
    for s in range(species):
        grid_a[s * rows : s * rows + levels, 0:wide] = halo_l[s]
        grid_a[s * rows : s * rows + levels, wide + cols :] = halo_r[s]
    span = cols + 2 * wide
    tables = (
        (adj_l[...] - HALO + wide - cols, blend_l[...]),
        (adj[...] - HALO + wide, blend[...]),
        (adj_r[...] - HALO + wide + cols, blend_r[...]),
    )
    table = jnp.concatenate([t[0] for t in tables], axis=1)
    weight = jnp.concatenate([t[1] for t in tables], axis=1)
    total = jnp.sum(weight, axis=0, keepdims=True)
    width = 256
    windows = []
    for b in range(span // width):
        low, high = max(0, width * b - LANES), min(span, width * (b + 1) + LANES)
        windows.append((low, high))
        source = iota((high - low, width), 0) + low
        matrix = jnp.zeros((high - low, width), jnp.float32)
        here = slice(width * b, width * (b + 1))
        for k in range(table.shape[0]):
            matrix = matrix + jnp.where(table[k : k + 1, here] == source, weight[k : k + 1, here], 0.0)
        hi, lo = halves(matrix)
        mix_hi[b, 0 : high - low, :] = hi
        mix_lo[b, 0 : high - low, :] = lo
    lines = species * rows

    def mix(step):
        old, new = (grid_a, grid_b) if step % 2 == 0 else (grid_b, grid_a)
        hi, lo = halves(old[...])
        pair[0:lines, :] = hi
        pair[lines:, :] = lo
        blocks = range(span // width)
        if step == STEPS - 1:
            blocks = range(wide // width, (wide + cols) // width)
        for b in blocks:
            low, high = windows[b]
            here = slice(width * b, width * (b + 1))
            both = mm(pair[:, low:high], mix_hi[b, 0 : high - low, :])
            update = both[0:lines] + both[lines:]
            update = update + mm(pair[0:lines, low:high], mix_lo[b, 0 : high - low, :])
            centre = old[:, here]
            new[:, here] = centre + (update - total[:, here] * centre)
        return new

    for step in range(STEPS - 1):
        mix(step)

    gpoints = emission.shape[1]
    strata = opacity.shape[2]
    for b in range(strata // LEVEL_BLOCK):
        for k in range(species):
            opac[b, k * gpoints : (k + 1) * gpoints, 0:LEVEL_BLOCK] = opacity[
                k, :, b * LEVEL_BLOCK : (b + 1) * LEVEL_BLOCK
            ]
    diagonal = iota((gpoints, gpoints), 0) == iota((gpoints, gpoints), 1)
    share = jnp.sum(jnp.where(diagonal, emission[...], 0.0), axis=1, keepdims=True)
    sunny = jnp.sum(jnp.where(diagonal, sunshine[...], 0.0), axis=1, keepdims=True)
    share = jnp.broadcast_to(share, (gpoints, rads))
    member = one_hot(iota((rads, cols), 0) == lax.shift_right_logical(memb[...], 2))

    for copy in copies:
        copy.wait()
    whole = recv[...]
    parts = [whole[:, 0:per, :].reshape(cols, LANES), whole[:, per : 2 * per, :].reshape(cols, LANES)]
    tail = whole[:, 2 * per :, :]
    big_block = iota((n, pack, LANES), 2) // 32
    tail = jnp.stack([jnp.where(big_block == q, tail, 0.0) for q in range(4)], axis=1)
    parts.append(tail.reshape(cols, LANES))
    across = []
    for k, part in enumerate(parts):
        hi, lo = halves(part)
        pooled[side, k] = (mm(member, hi) + mm(member, lo)) * 0.25
        copy = remote(
            pooled.at[side, k], pooled.at[side, k], ps_sem.at[k], pr_sem.at[k], {"sec": 1 - side}
        )
        copy.start()
        across.append(copy)

    def unfold(h):
        tail = pooled[h, 2].T
        tail = tail[0:32] + tail[32:64] + tail[64:96] + tail[96:128]
        field = jnp.concatenate([pooled[h, 0].T, pooled[h, 1].T, tail], axis=0)
        for k in range(2 + species):
            state[k, h, 0:levels, :] = field[k * rows : k * rows + levels]
        return field[levels : levels + 3]

    surface = unfold(side)
    for copy in across:
        copy.wait()
    unfold(1 - side)

    def fourth(value):
        square = value * value
        return square * square

    def gsum(value):
        return jnp.sum(value.reshape(gpoints // 8, 8, rads), axis=0)

    slant = -1.0 / surface[1:2]
    state[0, :, 0:levels, :] = fourth(state[0, :, 0:levels, :])

    def down(b, fluxes):
        thermal, direct = fluxes
        coeffs = opac[b]
        for i in range(LEVEL_BLOCK):
            level = b * LEVEL_BLOCK + i
            half = level // levels
            tau = None
            for k in range(species):
                part = coeffs[k * gpoints : (k + 1) * gpoints, i : i + 1] * state[2 + k, half, pl.ds(level - half * levels, 1), :]
                tau = part if tau is None else tau + part
            transmit = jnp.exp(-DIFFUSE * tau)
            trans[level] = transmit
            source = share * state[0, half, pl.ds(level - half * levels, 1), :]
            thermal = source + transmit * (thermal - source)
            direct = direct * jnp.exp(tau * slant)
            net[level + 1] = gsum(thermal + direct)
        return thermal, direct

    direct = sunny * surface[2:3]
    net[0] = gsum(direct)
    lax.fori_loop(0, strata // LEVEL_BLOCK, down, (jnp.zeros((gpoints, rads), jnp.float32), direct))
    upward = share * fourth(surface[0:1])
    net[strata] = net[strata] - gsum(upward)

    def up(b, upward):
        for i in range(LEVEL_BLOCK):
            level = strata - 1 - (b * LEVEL_BLOCK + i)
            half = level // levels
            source = share * state[0, half, pl.ds(level - half * levels, 1), :]
            upward = source + trans[level] * (upward - source)
            net[level] = net[level] - gsum(upward)
        return upward

    lax.fori_loop(0, strata // LEVEL_BLOCK, up, upward)
    heat[...] = jnp.zeros_like(heat)
    for h in range(2):
        change = net[h * levels : (h + 1) * levels] - net[h * levels + 1 : (h + 1) * levels + 1]
        heat[h, 0:levels] = jnp.sum(change, axis=1) / state[1, h, 0:levels, :]
    copy = remote(heat.at[1 - side], other, ts_sem, tr_sem, {"sec": 1 - side})
    copy.start()
    copy.wait()
    own = heat[side] + other[...]
    fold = per // 2
    hi, lo = halves(jnp.concatenate([own, own], axis=0))
    spread = (mm(hi, member) + mm(lo, member)).T.reshape(n, 2, fold, LANES)
    back[...] = jnp.where(iota((n, fold, LANES), 2) // 64 == 0, spread[:, 0], spread[:, 1])
    copies = []
    for d in [*range(n // 2, n), *range(n // 2 - 1, 0, -1)]:
        peer = flipped(me, d)
        copy = remote(back.at[peer], home.at[me], bo_sem.at[d], bi_sem.at[d], {"grp": peer})
        copy.start()
        copies.append(copy)
    home[me] = back[me]
    place = iota((n * fold, cols), 0)
    place = (place // fold) * (2 * fold) + lax.rem(place, fold) - pos[...]
    hots = [one_hot(place + q * fold == 0) for q in range(2)]
    last = mix(STEPS - 1)
    for s in range(species):
        mixed_out[s] = last[s * rows : s * rows + levels, wide : wide + cols]
    for copy in copies:
        copy.wait()
    value = home[...].reshape(n * fold, LANES).T
    hi, lo = halves(value)
    heats = None
    for q in range(2):
        here = slice(64 * q, 64 * (q + 1))
        part = mm(hi[here], hots[q]) + mm(lo[here], hots[q])
        heats = part if heats is None else heats + part
    heating[...] = heats[0:levels]


def one_kernel(n, *args):
    absorb = args[2]
    species, levels, cols = absorb.shape
    rows = -(-(levels + 3) // 8) * 8
    per = cols // n
    slab = 2 * per + per // 4
    wide = STEPS * HALO
    near = args[8].shape[0]
    gpoints, strata = args[10].shape[1:]
    span = cols + 2 * wide
    dma = pltpu.SemaphoreType.DMA
    f32 = jnp.float32
    return pl.pallas_call(
        functools.partial(device_kernel, n),
        out_shape=(
            jax.ShapeDtypeStruct((levels, cols), f32),
            jax.ShapeDtypeStruct(absorb.shape, f32),
        ),
        in_specs=[VMEM] * len(args),
        out_specs=(VMEM, VMEM),
        scratch_shapes=[
            pltpu.VMEM((3 * LANES, cols), f32),
            pltpu.VMEM((n, slab, LANES), f32),
            pltpu.VMEM((n, slab, LANES), f32),
            pltpu.VMEM((species, levels, wide), f32),
            pltpu.VMEM((species, levels, wide), f32),
            pltpu.VMEM((near, wide), jnp.int32),
            pltpu.VMEM((near, wide), jnp.int32),
            pltpu.VMEM((near, wide), f32),
            pltpu.VMEM((near, wide), f32),
            pltpu.VMEM((species * rows, span), f32),
            pltpu.VMEM((species * rows, span), f32),
            pltpu.VMEM((span // 256, 512, 256), jnp.bfloat16),
            pltpu.VMEM((span // 256, 512, 256), jnp.bfloat16),
            pltpu.VMEM((2, 3, cols // 4, LANES), f32),
            pltpu.VMEM((2 + species, 2, rows, cols // 4), f32),
            pltpu.VMEM((strata // LEVEL_BLOCK, species * gpoints, LANES), f32),
            pltpu.VMEM((strata, gpoints, cols // 4), f32),
            pltpu.VMEM((strata + 1, 8, cols // 4), f32),
            pltpu.VMEM((2, 64, cols // 4), f32),
            pltpu.VMEM((64, cols // 4), f32),
            pltpu.VMEM((n, per // 2, LANES), f32),
            pltpu.VMEM((n, per // 2, LANES), f32),
            pltpu.VMEM((2 * species * rows, span), jnp.bfloat16),
            dma((n,)), dma((n,)), dma((6,)), dma((6,)), dma((3,)), dma((3,)), dma, dma, dma((n,)), dma((n,)),
        ],
        compiler_params=pltpu.CompilerParams(
            collective_id=0, has_side_effects=True, vmem_limit_bytes=48 << 20
        ),
        cost_estimate=pl.CostEstimate(flops=10**9, bytes_accessed=4 << 20, transcendentals=10**6),
    )(*args)


def folds_evenly(n, sides, levels, cols, species, gpoints):
    rows = -(-(levels + 3) // 8) * 8
    return (
        n > 7 and n & (n - 1) == 0 and sides == 2 and species == 4
        and cols == n * 32 and cols == 4 * LANES and 2 * STEPS * HALO == cols
        and 6 * rows == 2 * LANES + 32 and gpoints % 8 == 0 and 2 * levels % LEVEL_BLOCK == 0
    )


def per_device(*args):
    (warmth, depth, absorb, ground, sun, mask, pos, memb, adj, blend, opacity, emission, sunshine) = args
    n = lax.axis_size("grp")
    levels, cols = warmth.shape
    gpoints = emission.shape[0]
    if not folds_evenly(n, lax.axis_size("sec"), levels, cols, absorb.shape[0], gpoints):
        return plain_device(*args)
    return one_kernel(
        n, warmth, depth, absorb, ground[None], sun[None], mask[None], pos, memb, adj, blend,
        opacity, emission[None], sunshine[None],
    )


def solution(mesh):
    in_specs = (
        P("sec", "grp"),
        P("sec", "grp"),
        P(None, "sec", "grp"),
        P("grp"),
        P("grp"),
        P("grp"),
        P("grp", None),
        P("grp", None),
        P(None, "grp"),
        P(None, "grp"),
        P(None, "sec", None),
        P("sec"),
        P("sec"),
    )
    out_specs = (P("sec", "grp"), P(None, "sec", "grp"))
    return jax.shard_map(
        per_device, mesh=mesh, in_specs=in_specs, out_specs=out_specs, check_vma=False
    )
```
